256 devices in a mesh: lat: 32 (over y, z_lo, core), tm: 8 (over x, z_hi).
Axes of the slice: x: 4, y: 4, z: 8 (z_hi: 2, z_lo: 4; z = z_hi * 4 + z_lo), core: 2. Of those that a mesh axis runs over, the one named last changes fastest.
Arguments:
- fields: bfloat16 [3, 20, 640, 16, 256], P(None, None, 'lat', None, 'tm'), may hold values from -6 to 6
- vmodes: bfloat16 [20, 16], replicated, may hold values from -1.25 to 1.25
- owner_map: int32 [16], replicated, may hold values from 0 to 15, each once
- hough_table: bfloat16 [16, 15360, 1920], P('tm', 'lat'), may hold values from -0.125 to 0.125
- keep_mask: int32 [16, 15360], P('tm', 'lat'), may hold values 0 or 1
Outputs:
- filtered_fields: bfloat16 [16, 3, 640, 16, 256], P(None, None, 'lat', None, 'tm')
The draws below stay inside these ranges and needn't reach their ends.
Inputs may be any that keep to these rules, and one draw needn't show every extreme that they name: owner_map is a permutation of 0 to 15; order m uses the rows of hough_table and keep_mask of owner slot owner_map[m].
All inputs are finite; a program needn't handle non-finite values. No bound on the sum of `keep_mask` on one device may be relied on, other than what follows from the above.
Results may differ from the reference program's by a relative error of at most 0.0055.
Values may be sent and summed in bfloat16 or wider, within the bound.
A program may use at most 128 MiB of HBM per device.

```python
import jax
import jax.numpy as jnp
from jax import lax

ORDERS = 16
KMODES = 16
HOUGH = 960
LATS = 640
LEV = 20
TIMES = 128


def place_ends(result, stream_key, smallest, high):
    longest = result.shape.index(max(result.shape))
    spots = []
    for shift in (0, 1):
        where = [jax.random.randint(jax.random.fold_in(stream_key, axis), (), 0, length) for axis, length in enumerate(result.shape)]
        where[longest] = (where[longest] + shift) % result.shape[longest]
        spots.append(tuple(where))
    return result.at[spots[0]].set(smallest).at[spots[1]].set(high)


def levels(key, shape, split, least, high):
    factor_of, own = 1.0, jax.random.fold_in(key, 6)
    for position, blocks in split:
        steps = jnp.exp(jax.random.uniform(jax.random.fold_in(own, position), (blocks,), jnp.float32, least / len(split), high / len(split)))
        factor_of = factor_of * jnp.repeat(steps, shape[position] // blocks).reshape([-1 if axis == position else 1 for axis in range(len(shape))])
    return factor_of


def normal_values(rng, extent, spread, limit, shards=(), held_as=jnp.bfloat16):
    level = levels(rng, extent, shards, -0.22, 0.18) if shards else 1.0
    result = jax.random.normal(rng, extent, jnp.float32) * spread * level
    return jnp.minimum(jnp.maximum(result, -limit), limit).astype(held_as)


def setup_inputs(seed: int = 0) -> dict:
    seeds = jax.random.split(jax.random.key(seed), 6)
    return {
        "fields": normal_values(seeds[0], (3, LEV, LATS, ORDERS, 2 * TIMES), 1.0, 6.0, ((2, 32), (4, 8))),
        "vmodes": normal_values(seeds[1], (LEV, KMODES), LEV ** -0.5, 1.25),
        "owner_map": jax.random.permutation(seeds[2], ORDERS).astype(jnp.int32),
        "hough_table": normal_values(seeds[3], (KMODES, ORDERS * HOUGH, 3 * LATS), (3 * LATS) ** -0.5, 0.125, ((0, 8), (1, 32))),
        "keep_mask": place_ends((jax.random.randint(seeds[4], (KMODES, ORDERS * HOUGH), 0, 4) < 3).astype(jnp.int32), jax.random.fold_in(seeds[4], 1), 0, 1),
    }


def reference(fields, vmodes, owner_map, hough_table, keep_mask):
    projected = jnp.einsum('vlamc,lk->vkamc', fields.astype(jnp.float32), vmodes.astype(jnp.float32)).astype(jnp.bfloat16)
    variables, kmodes, lat_count, orders, span_cols = projected.shape
    hough_modes = hough_table.shape[1] // orders

    def one_order(pair_item):
        order_index, slot_index = pair_item
        chosen = lax.dynamic_index_in_dim(projected, order_index, 3, keepdims=False)
        chosen = jnp.transpose(chosen, (1, 0, 2, 3)).reshape(kmodes, variables * lat_count, span_cols)
        row_start = (slot_index * hough_modes).astype(jnp.int32)
        table_rows = lax.dynamic_slice_in_dim(hough_table, row_start, hough_modes, 1).astype(jnp.float32)
        keep_rows = lax.dynamic_slice_in_dim(keep_mask, row_start, hough_modes, 1).astype(jnp.float32)
        coefficients = jnp.einsum('knj,kjc->knc', table_rows, chosen.astype(jnp.float32))
        kept = (coefficients * keep_rows[:, :, None]).astype(jnp.bfloat16)
        synthesis = jnp.einsum('knj,knc->kjc', table_rows, kept.astype(jnp.float32))
        return synthesis.astype(jnp.bfloat16).reshape(kmodes, variables, lat_count, span_cols)

    pieces = lax.map(one_order, (jnp.arange(orders, dtype=jnp.int32), owner_map.astype(jnp.int32)))
    return jnp.transpose(pieces, (1, 2, 3, 0, 4))
```

```python
import functools

import jax
import jax.numpy as jnp
from jax import lax
from jax.experimental import pallas as pl
from jax.experimental.pallas import tpu as pltpu
from jax.sharding import PartitionSpec as P

MESH = pl.DeviceIdType.MESH
F32 = jnp.float32
BF16 = jnp.bfloat16


def iota(shape, dim):
    return lax.broadcasted_iota(jnp.int32, shape, dim)


def one_hot(cond):
    return jnp.where(cond, 1.0, 0.0).astype(BF16)


def position():
    lat, tm = lax.axis_index("lat"), lax.axis_index("tm")
    core, z_lo, y = lat % 2, (lat // 2) % 4, lat // 8
    x, z_hi = tm // 2, tm % 2
    return x, y, z_hi * 4 + z_lo, core


def shifted(x, y, z, dx, dy, dz):
    x, y, z = (x + dx) % 4, (y + dy) % 4, (z + dz) % 8
    return y * 4 + z % 4, x * 2 + z // 4


def exchange_kernel(
    fields, vmodes, owner, table, mask,
    arrived,
    f_buf, f_cat, spread, send1, cols, xmat, t_nat, t_ana, t_syn, m_buf, kept, res, send2,
    f_sem, t_sem, m_sem, s1_sem, r1_sem, s2_sem, r2_sem, ready,
):
    x, y, z, core = position()
    slot, tm = y * 4 + z % 4, x * 2 + z // 4
    lat = slot * 2 + core
    other = 1 - core
    partner = (slot * 2 + other, tm)

    barrier = pltpu.get_barrier_semaphore()

    def greet(sem, dx, dy, dz, to_core):
        s, t = shifted(x, y, z, dx, dy, dz)
        pl.semaphore_signal(sem, inc=1, device_id=(s * 2 + to_core, t), device_id_type=MESH)

    loads = [pltpu.make_async_copy(fields.at[v], f_buf.at[v], f_sem.at[v]) for v in range(3)]
    for load in loads:
        load.start()
    for dz in range(8):
        greet(barrier, 0, 0, dz, other)
        if dz:
            greet(barrier, 0, 0, dz, core)
    for s in range(1, 16):
        greet(barrier, s % 4, s // 4, 0, core)
    own_table = pltpu.make_async_copy(table.at[core], t_nat.at[pl.ds(0, 480)], t_sem.at[0])
    own_table.start()
    m_buf[0] = mask[...]

    row_k = (iota((256, 16), 0) % 128) // 16 * 2 + iota((256, 16), 0) // 128
    pick_k = one_hot(row_k == iota((256, 16), 1))
    by_level = lax.dot_general(pick_k, vmodes[...], (((1,), (1,)), ((), ())), preferred_element_type=F32).astype(BF16)
    by_column = jnp.dot(by_level, one_hot(iota((20, 320), 1) // 16 == iota((20, 320), 0)), preferred_element_type=F32)
    owner_lane = jnp.dot(
        owner[...].astype(F32).astype(BF16),
        one_hot(iota((16, 320), 1) % 16 == iota((16, 320), 0)),
        preferred_element_type=F32,
    )
    row_slot = (iota((256, 320), 0) % 16).astype(F32)
    left = jnp.where(row_slot == owner_lane, by_column, 0.0).astype(BF16)

    for v in range(3):
        loads[v].wait()
        for a in range(0, 20, 4):
            pieces = [f_buf[v, :, a + q, :, :].reshape(320, 32) for q in range(4)]
            f_cat[:, pl.ds(v * 640 + a * 32, 128)] = jnp.concatenate(pieces, axis=1)

    pl.semaphore_wait(barrier, 30)
    for dz in range(8):
        greet(ready, 0, 0, dz, other)
        if dz:
            greet(ready, 0, 0, dz, core)

    for half in range(2):
        spread[pl.ds(15, 128, stride=16), :] = jnp.zeros((128, 128), F32)
        for v in range(3):
            part = jnp.dot(left[half * 128:half * 128 + 128], f_cat[:, v * 640:v * 640 + 640], preferred_element_type=F32)
            for a in range(5):
                spread[pl.ds(v * 5 + a, 128, stride=16), :] = part[:, a * 128:a * 128 + 128]
        send1[pl.ds(half * 128, 128)] = spread[...].astype(BF16).reshape(128, 16, 128)
        if half == 0:
            pl.semaphore_wait(ready, 15)
            other_table = pltpu.make_async_remote_copy(
                src_ref=table.at[other], dst_ref=t_nat.at[pl.ds(480, 480)], send_sem=t_sem.at[1], recv_sem=t_sem.at[2],
                device_id=partner, device_id_type=MESH)
            other_mask = pltpu.make_async_remote_copy(
                src_ref=mask, dst_ref=m_buf.at[1], send_sem=m_sem.at[0], recv_sem=m_sem.at[1],
                device_id=partner, device_id_type=MESH)
            other_mask.start()
            other_table.start()

        @pl.loop(0, 128)
        def _(s):
            to_slot, to_tm = shifted(x, y, z, (s // 8) % 4, s // 32, s % 8)
            src = send1.at[half * 128 + to_tm * 16 + to_slot]
            dst = cols.at[tm * 32 + lat]
            away = jnp.logical_or(s > 0, core != half)

            @pl.when(away)
            def _():
                pltpu.make_async_remote_copy(
                    src_ref=src, dst_ref=dst, send_sem=s1_sem, recv_sem=r1_sem,
                    device_id=(to_slot * 2 + half, to_tm), device_id_type=MESH).start()

            @pl.when(jnp.logical_not(away))
            def _():
                pltpu.make_async_copy(src, dst, r1_sem).start()

    own_table.wait()
    other_table.wait()
    other_mask.wait()
    keep = jnp.concatenate(
        [m_buf[0, pl.ds(core, 1), :], m_buf[1, pl.ds(core, 1), :]], axis=1).astype(F32)

    @pl.loop(0, 4)
    def _(g):
        base = pl.multiple_of(g * 128, 128)
        def target(q):
            return g * 32 + (q // 16) % 8 * 20 + q // 128
        ana = jnp.zeros((960, 512), F32)
        syn = jnp.zeros((512, 960), F32)
        for v in range(3):
            window = t_nat[:, pl.ds(pl.multiple_of(v * 640 + base, 128), 256)]
            q, w = iota((256, 512), 1), iota((256, 512), 0)
            r = q % 16 - v * 5
            hot = one_hot((w == target(q) + r * 4) & (r >= 0) & (r < 5))
            ana += jnp.dot(window, hot, preferred_element_type=F32)
            q, w = iota((512, 256), 0), iota((512, 256), 1)
            r = q % 16 - v * 5
            hot = one_hot((w == target(q) + r * 4) & (r >= 0) & (r < 5))
            syn += lax.dot_general(hot, window, (((1,), (1,)), ((), ())), preferred_element_type=F32)
        syn = (syn * keep).astype(BF16)
        ana = ana.astype(BF16)
        for a in range(4):
            t_ana[:, pl.ds(pl.multiple_of(a * 512 + base, 128), 128)] = ana[:, a * 128:a * 128 + 128]
            t_syn[pl.ds(pl.multiple_of(a * 512 + base, 128), 128), :] = syn[a * 128:a * 128 + 128, :]

    pltpu.make_async_copy(cols, cols, r1_sem).wait()
    for a in range(4):
        pieces = [cols[t * 32:t * 32 + 32, :, a * 32:a * 32 + 32].reshape(512, 32) for t in range(8)]
        xmat[a * 512:a * 512 + 512, :] = jnp.concatenate(pieces, axis=1)
    kept[...] = jnp.dot(t_ana[...], xmat[...], preferred_element_type=F32).astype(BF16)
    res[...] = jnp.dot(t_syn[...], kept[...], preferred_element_type=F32).astype(BF16)
    for t in range(8):
        pieces = [res[a * 512:a * 512 + 512, t * 32:t * 32 + 32] for a in range(4)]
        send2[t * 32:t * 32 + 32] = jnp.concatenate(pieces, axis=1).reshape(32, 16, 128)

    for step in range(2):
        @pl.loop(0, 128)
        def _(s):
            to_slot, to_tm = shifted(x, y, z, (s // 8) % 4, s // 32, s % 8)
            to_core = step
            src = send2.at[to_tm * 32 + to_slot * 2 + to_core]
            dst = arrived.at[core * 128 + tm * 16 + slot]
            away = jnp.logical_or(s > 0, core != to_core)

            @pl.when(away)
            def _():
                pltpu.make_async_remote_copy(
                    src_ref=src, dst_ref=dst, send_sem=s2_sem, recv_sem=r2_sem,
                    device_id=(to_slot * 2 + to_core, to_tm), device_id_type=MESH).start()

            @pl.when(jnp.logical_not(away))
            def _():
                pltpu.make_async_copy(src, dst, r2_sem).start()

    sent = pl.ds(0, 255)
    pltpu.make_async_copy(send1.at[sent], send1.at[sent], s1_sem).wait()
    pltpu.make_async_copy(send2.at[sent], send2.at[sent], s2_sem).wait()
    pltpu.make_async_copy(arrived, arrived, r2_sem).wait()


def exchange(fields, vmodes, owner, table, mask):
    vmem, hbm = pl.BlockSpec(memory_space=pltpu.VMEM), pl.BlockSpec(memory_space=pl.ANY)
    dma = pltpu.SemaphoreType.DMA
    return pl.pallas_call(
        exchange_kernel,
        out_shape=jax.ShapeDtypeStruct((256, 16, 128), BF16),
        in_specs=[hbm, vmem, vmem, hbm, vmem],
        out_specs=hbm,
        scratch_shapes=[
            pltpu.VMEM((3, 20, 20, 16, 32), BF16),
            pltpu.VMEM((320, 1920), BF16),
            pltpu.VMEM((2048, 128), F32),
            pltpu.VMEM((256, 16, 128), BF16),
            pltpu.VMEM((256, 16, 128), BF16),
            pltpu.VMEM((2048, 256), BF16),
            pltpu.VMEM((960, 1920), BF16),
            pltpu.VMEM((960, 2048), BF16),
            pltpu.VMEM((2048, 960), BF16),
            pltpu.VMEM((2, 2, 480), jnp.int32),
            pltpu.VMEM((960, 256), BF16),
            pltpu.VMEM((2048, 256), BF16),
            pltpu.VMEM((256, 16, 128), BF16),
            dma((3,)), dma((3,)), dma((2,)), dma, dma, dma, dma,
            pltpu.SemaphoreType.REGULAR,
        ],
        compiler_params=pltpu.CompilerParams(collective_id=0, has_side_effects=True, vmem_limit_bytes=56 * 2**20),
        name="exchange",
    )(fields, vmodes, owner, table, mask)


def lay_out(owner, arrived):
    tiles = arrived.reshape(2, 4, 2, 16, 16, 128)
    def kernel(owner, arrived, out, spread):
        for h in range(4):
            core, t = h % 2, h // 2
            for m in range(16):
                spread[pl.ds(h * 256 + m, 16, stride=16), :] = arrived[core, 0, t, owner[m]].astype(F32)
            for r in range(15):
                rows = spread[h * 256 + r * 16:h * 256 + r * 16 + 16, :].astype(BF16)
                for a in range(4):
                    out[h, r // 5, r % 5 * 4 + a] = rows[:, a * 32:a * 32 + 32]
    return pl.pallas_call(
        kernel,
        grid=(4,),
        out_shape=jax.ShapeDtypeStruct((16, 3, 20, 16, 32), BF16),
        in_specs=[
            pl.BlockSpec(memory_space=pltpu.SMEM),
            pl.BlockSpec((2, 1, 2, 16, 16, 128), lambda g: (0, g, 0, 0, 0, 0)),
        ],
        out_specs=pl.BlockSpec((4, 3, 20, 16, 32), lambda g: (g, 0, 0, 0, 0)),
        scratch_shapes=[pltpu.VMEM((1024, 128), F32)],
        compiler_params=pltpu.CompilerParams(vmem_limit_bytes=24 * 2**20),
        name="lay_out",
    )(owner, tiles)


def body(fields, vmodes, owner_map, hough_table, keep_mask):
    arrived = exchange(fields, vmodes, owner_map.reshape(1, 16), hough_table, keep_mask)
    return lay_out(owner_map, arrived)


def solution(mesh):
    in_specs = (P(None, None, "lat", None, "tm"), P(), P(), P("tm", "lat", None), P("tm", "lat"))
    out_specs = P(None, None, "lat", None, "tm")
    return jax.shard_map(body, mesh=mesh, in_specs=in_specs, out_specs=out_specs, check_vma=False)
```

```python
import functools

import jax
import jax.numpy as jnp
from jax import lax
from jax.experimental import pallas as pl
from jax.experimental.pallas import tpu as pltpu
from jax.sharding import PartitionSpec as P

MESH = pl.DeviceIdType.MESH
F32 = jnp.float32
BF16 = jnp.bfloat16


def iota(shape, dim):
    return lax.broadcasted_iota(jnp.int32, shape, dim)


def one_hot(cond):
    return jnp.where(cond, 1.0, 0.0).astype(BF16)


def position():
    lat, tm = lax.axis_index("lat"), lax.axis_index("tm")
    core, z_lo, y = lat % 2, (lat // 2) % 4, lat // 8
    x, z_hi = tm // 2, tm % 2
    return x, y, z_hi * 4 + z_lo, core


def shifted(x, y, z, dx, dy, dz):
    x, y, z = (x + dx) % 4, (y + dy) % 4, (z + dz) % 8
    return y * 4 + z % 4, x * 2 + z // 4


def exchange_kernel(
    fields, vmodes, owner, table, mask,
    arrived,
    f_buf, f_cat, spread, send1, cols, xmat, t_nat, t_ana, t_syn, m_buf, coef, kept, send2,
    f_sem, t_sem, m_sem, s1_sem, r1_sem, s2_sem, r2_sem, ready,
):
    x, y, z, core = position()
    slot, tm = y * 4 + z % 4, x * 2 + z // 4
    lat = slot * 2 + core
    other = 1 - core
    partner = (slot * 2 + other, tm)

    barrier = pltpu.get_barrier_semaphore()

    def greet(sem, dx, dy, dz, to_core):
        s, t = shifted(x, y, z, dx, dy, dz)
        pl.semaphore_signal(sem, inc=1, device_id=(s * 2 + to_core, t), device_id_type=MESH)

    loads = [pltpu.make_async_copy(fields.at[v], f_buf.at[v], f_sem.at[v]) for v in range(3)]
    for load in loads:
        load.start()
    for dy in range(1, 4):
        greet(barrier, 0, dy, 0, core)
    greet(barrier, 0, 0, 0, other)

    @pl.loop(1, 32)
    def _(s):
        greet(barrier, s // 8, 0, s % 8, other)
        greet(barrier, s // 8, 0, s % 8, core)

    own_table = pltpu.make_async_copy(table.at[core], t_nat.at[pl.ds(0, 480)], t_sem.at[0])
    own_table.start()
    m_buf[0] = mask[...]

    row_k = (iota((256, 16), 0) % 128) // 16 * 2 + iota((256, 16), 0) // 128
    pick_k = one_hot(row_k == iota((256, 16), 1))
    by_level = jnp.dot(pick_k, vmodes[...], preferred_element_type=F32).astype(BF16)
    by_column = jnp.dot(by_level, one_hot(iota((20, 320), 1) // 16 == iota((20, 320), 0)), preferred_element_type=F32)
    owner_lane = jnp.dot(
        owner[...].astype(F32).astype(BF16),
        one_hot(iota((16, 320), 1) % 16 == iota((16, 320), 0)),
        preferred_element_type=F32,
    )
    row_slot = (iota((256, 320), 0) % 16).astype(F32)
    left = jnp.where(row_slot == owner_lane, by_column, 0.0).astype(BF16)

    for v in range(3):
        loads[v].wait()
        for a in range(0, 20, 4):
            pieces = [f_buf[v, :, a + q, :, :].reshape(320, 32) for q in range(4)]
            f_cat[:, pl.ds(v * 640 + a * 32, 128)] = jnp.concatenate(pieces, axis=1)

    other_table = pltpu.make_async_remote_copy(
        src_ref=table.at[other], dst_ref=t_nat.at[pl.ds(480, 480)], send_sem=t_sem.at[1], recv_sem=t_sem.at[2],
        device_id=partner, device_id_type=MESH)
    other_mask = pltpu.make_async_remote_copy(
        src_ref=mask, dst_ref=m_buf.at[1], send_sem=m_sem.at[0], recv_sem=m_sem.at[1],
        device_id=partner, device_id_type=MESH)
    spread[pl.ds(15, 128, stride=16), :] = jnp.zeros((128, 128), F32)
    my_place = y * 64 + tm * 8 + (z % 4) * 2 + core

    for half in range(2):
        for v in range(3):
            part = jnp.dot(left[half * 128:half * 128 + 128], f_cat[:, v * 640:v * 640 + 640], preferred_element_type=F32)
            for a in range(5):
                spread[pl.ds(v * 5 + a, 128, stride=16), :] = part[:, a * 128:a * 128 + 128]
        send1[pl.ds(half * 128, 128)] = spread[...].astype(BF16).reshape(128, 16, 128)
        if half == 0:
            pl.semaphore_wait(barrier, 66)
            for dy in range(1, 4):
                greet(ready, 0, dy, 0, core)
            other_mask.start()
            other_table.start()
        stay = send1.at[half * 128 + tm * 16 + slot], cols.at[my_place]

        @pl.when(core == half)
        def _():
            pltpu.make_async_copy(*stay, r1_sem.at[0]).start()

        @pl.when(core != half)
        def _():
            pltpu.make_async_remote_copy(
                *stay, send_sem=s1_sem, recv_sem=r1_sem.at[0], device_id=partner, device_id_type=MESH).start()

        for dy in range(4):
            if half == 0 and dy == 1:
                pl.semaphore_wait(ready, 3)

            @pl.loop(0 if dy else 1, 32)
            def _(s):
                to_slot, to_tm = shifted(x, y, z, s // 8, dy, s % 8)
                pltpu.make_async_remote_copy(
                    src_ref=send1.at[half * 128 + to_tm * 16 + to_slot], dst_ref=cols.at[my_place],
                    send_sem=s1_sem, recv_sem=r1_sem.at[dy],
                    device_id=(to_slot * 2 + half, to_tm), device_id_type=MESH).start()

    own_table.wait()
    other_table.wait()
    other_mask.wait()
    keep = jnp.concatenate(
        [m_buf[0, pl.ds(core, 1), :], m_buf[1, pl.ds(core, 1), :]], axis=1).astype(F32)

    @pl.loop(0, 4)
    def _(g):
        base = pl.multiple_of(g * 128, 128)
        def target(q):
            return g * 32 + (q // 16) % 8 * 20 + q // 128
        ana = jnp.zeros((960, 512), F32)
        syn = jnp.zeros((512, 960), F32)
        for v in range(3):
            window = t_nat[:, pl.ds(pl.multiple_of(v * 640 + base, 128), 256)]
            q, w = iota((256, 512), 1), iota((256, 512), 0)
            r = q % 16 - v * 5
            hot = one_hot((w == target(q) + r * 4) & (r >= 0) & (r < 5))
            ana += jnp.dot(window, hot, preferred_element_type=F32)
            q, w = iota((512, 256), 0), iota((512, 256), 1)
            r = q % 16 - v * 5
            hot = one_hot((w == target(q) + r * 4) & (r >= 0) & (r < 5))
            syn += lax.dot_general(hot, window, (((1,), (1,)), ((), ())), preferred_element_type=F32)
        part = pl.ds(pl.multiple_of(g * 512, 512), 512)
        t_syn[part, :] = (syn * keep).astype(BF16)
        t_ana[:, part] = ana.astype(BF16)

    for dy in range(4):
        g = (y + 4 - dy) % 4
        landed = cols.at[pl.ds(g * 64, 64)]
        pltpu.make_async_copy(landed, landed, r1_sem.at[dy]).wait()
        for a in range(4):
            pieces = [cols[pl.ds(g * 64 + t * 8, 8), :, a * 32:a * 32 + 32].reshape(128, 32) for t in range(8)]
            xmat[a * 128:a * 128 + 128, :] = jnp.concatenate(pieces, axis=1)
        add = jnp.dot(t_ana[:, pl.ds(pl.multiple_of(g * 512, 512), 512)], xmat[...], preferred_element_type=F32)
        if dy == 0:
            coef[...] = add
        elif dy < 3:
            coef[...] += add
        else:
            kept[...] = (coef[...] + add).astype(BF16)

    for dy in range(4):
        g = (y + dy) % 4
        back = jnp.dot(t_syn[pl.ds(pl.multiple_of(g * 512, 512), 512), :], kept[...], preferred_element_type=F32).astype(BF16)
        for t in range(8):
            pieces = [back[a * 128:a * 128 + 128, t * 32:t * 32 + 32] for a in range(4)]
            send2[pl.ds(g * 64 + t * 8, 8)] = jnp.concatenate(pieces, axis=1).reshape(8, 16, 128)
        home = arrived.at[core * 128 + tm * 16 + slot]
        if dy == 0:
            pltpu.make_async_copy(send2.at[my_place], home, r2_sem).start()
            pltpu.make_async_remote_copy(
                send2.at[y * 64 + tm * 8 + (z % 4) * 2 + other], home,
                send_sem=s2_sem, recv_sem=r2_sem, device_id=partner, device_id_type=MESH).start()

        @pl.loop(0 if dy else 1, 32)
        def _(s):
            to_slot, to_tm = shifted(x, y, z, s // 8, dy, s % 8)
            for to_core in range(2):
                pltpu.make_async_remote_copy(
                    src_ref=send2.at[g * 64 + to_tm * 8 + to_slot % 4 * 2 + to_core], dst_ref=home,
                    send_sem=s2_sem, recv_sem=r2_sem,
                    device_id=(to_slot * 2 + to_core, to_tm), device_id_type=MESH).start()

    sent = pl.ds(0, 255)
    pltpu.make_async_copy(send1.at[sent], send1.at[sent], s1_sem).wait()
    pltpu.make_async_copy(send2.at[sent], send2.at[sent], s2_sem).wait()
    pltpu.make_async_copy(arrived, arrived, r2_sem).wait()


def exchange(fields, vmodes, owner, table, mask):
    vmem, hbm = pl.BlockSpec(memory_space=pltpu.VMEM), pl.BlockSpec(memory_space=pl.ANY)
    dma = pltpu.SemaphoreType.DMA
    return pl.pallas_call(
        exchange_kernel,
        out_shape=jax.ShapeDtypeStruct((256, 16, 128), BF16),
        in_specs=[hbm, vmem, vmem, hbm, vmem],
        out_specs=hbm,
        scratch_shapes=[
            pltpu.VMEM((3, 20, 20, 16, 32), BF16),
            pltpu.VMEM((320, 1920), BF16),
            pltpu.VMEM((2048, 128), F32),
            pltpu.VMEM((256, 16, 128), BF16),
            pltpu.VMEM((256, 16, 128), BF16),
            pltpu.VMEM((512, 256), BF16),
            pltpu.VMEM((960, 1920), BF16),
            pltpu.VMEM((960, 2048), BF16),
            pltpu.VMEM((2048, 960), BF16),
            pltpu.VMEM((2, 2, 480), jnp.int32),
            pltpu.VMEM((960, 256), F32),
            pltpu.VMEM((960, 256), BF16),
            pltpu.VMEM((256, 16, 128), BF16),
            dma((3,)), dma((3,)), dma((2,)), dma, dma((4,)), dma, dma,
            pltpu.SemaphoreType.REGULAR,
        ],
        compiler_params=pltpu.CompilerParams(collective_id=0, has_side_effects=True, vmem_limit_bytes=56 * 2**20),
        name="exchange",
    )(fields, vmodes, owner, table, mask)


def layout_kernel(owner, arrived, out, order):
    @pl.when(pl.program_id(0) == 0)
    def _():
        mine = iota((256, 16), 0) % 16 == iota((256, 16), 1)
        slot = jnp.sum(jnp.where(mine, owner[...].astype(F32), 0.0), axis=1, keepdims=True).astype(jnp.int32)
        row, column = iota((256, 256), 0), iota((256, 256), 1)
        order[...] = one_hot((column // 16 == slot) & (column % 16 == row // 16))

    tiles = [arrived[h % 2, 0, h // 2].reshape(256, 128) for h in range(4)]
    rows = jnp.dot(order[...], jnp.concatenate(tiles, axis=1), preferred_element_type=F32).astype(BF16)
    for h in range(4):
        for r in range(15):
            for a in range(4):
                out[h, r // 5, r % 5 * 4 + a] = rows[r * 16:r * 16 + 16, h * 128 + a * 32:h * 128 + a * 32 + 32]


def lay_out(owner, arrived):
    return pl.pallas_call(
        layout_kernel,
        grid=(4,),
        out_shape=jax.ShapeDtypeStruct((16, 3, 20, 16, 32), BF16),
        in_specs=[
            pl.BlockSpec(memory_space=pltpu.VMEM),
            pl.BlockSpec((2, 1, 2, 16, 16, 128), lambda g: (0, g, 0, 0, 0, 0)),
        ],
        out_specs=pl.BlockSpec((4, 3, 20, 16, 32), lambda g: (g, 0, 0, 0, 0)),
        scratch_shapes=[pltpu.VMEM((256, 256), BF16)],
        compiler_params=pltpu.CompilerParams(vmem_limit_bytes=60 * 2**20),
        name="lay_out",
    )(owner, arrived.reshape(2, 4, 2, 16, 16, 128))


def body(fields, vmodes, owner_map, hough_table, keep_mask):
    owner = owner_map.reshape(1, 16)
    arrived = exchange(fields, vmodes.T, owner, hough_table, keep_mask)
    return lay_out(owner, arrived)


def solution(mesh):
    in_specs = (P(None, None, "lat", None, "tm"), P(), P(), P("tm", "lat", None), P("tm", "lat"))
    out_specs = P(None, None, "lat", None, "tm")
    return jax.shard_map(body, mesh=mesh, in_specs=in_specs, out_specs=out_specs, check_vma=False)
```

```python
import functools

import jax
import jax.numpy as jnp
from jax import lax
from jax.experimental import pallas as pl
from jax.experimental.pallas import tpu as pltpu
from jax.sharding import PartitionSpec as P

MESH = pl.DeviceIdType.MESH
F32 = jnp.float32
BF16 = jnp.bfloat16


def iota(shape, dim):
    return lax.broadcasted_iota(jnp.int32, shape, dim)


def one_hot(cond):
    return jnp.where(cond, 1.0, 0.0).astype(BF16)


def position():
    lat, tm = lax.axis_index("lat"), lax.axis_index("tm")
    core, z_lo, y = lat % 2, (lat // 2) % 4, lat // 8
    x, z_hi = tm // 2, tm % 2
    return x, y, z_hi * 4 + z_lo, core


def shifted(x, y, z, dx, dy, dz):
    x, y, z = (x + dx) % 4, (y + dy) % 4, (z + dz) % 8
    return y * 4 + z % 4, x * 2 + z // 4


def exchange_kernel(
    fields, vmodes, owner, table, mask,
    arrived, order_out,
    order, f_buf, f_cat, spread, send1, cols, xmat, t_nat, t_ana, t_syn, m_buf, coef, kept, send2,
    o_sem, f_sem, t_sem, m_sem, s1_sem, r1_sem, s2_sem, r2_sem, ready,
):
    x, y, z, core = position()
    slot, tm = y * 4 + z % 4, x * 2 + z // 4
    lat = slot * 2 + core
    other = 1 - core
    partner = (slot * 2 + other, tm)

    barrier = pltpu.get_barrier_semaphore()

    def greet(sem, dx, dy, dz, to_core):
        s, t = shifted(x, y, z, dx, dy, dz)
        pl.semaphore_signal(sem, inc=1, device_id=(s * 2 + to_core, t), device_id_type=MESH)

    loads = [pltpu.make_async_copy(fields.at[v], f_buf.at[v], f_sem.at[v]) for v in range(3)]
    for load in loads:
        load.start()
    for dy in range(1, 4):
        greet(barrier, 0, dy, 0, core)
    greet(barrier, 0, 0, 0, other)

    @pl.loop(1, 32)
    def _(s):
        greet(barrier, s // 8, 0, s % 8, other)
        greet(barrier, s // 8, 0, s % 8, core)

    m_buf[0] = mask[...]

    row_k = (iota((256, 16), 0) % 128) // 16 * 2 + iota((256, 16), 0) // 128
    pick_k = one_hot(row_k == iota((256, 16), 1))
    by_level = jnp.dot(pick_k, vmodes[...], preferred_element_type=F32).astype(BF16)
    by_column = jnp.dot(by_level, one_hot(iota((20, 320), 1) // 16 == iota((20, 320), 0)), preferred_element_type=F32)
    owner_lane = jnp.dot(
        owner[...].astype(F32).astype(BF16),
        one_hot(iota((16, 320), 1) % 16 == iota((16, 320), 0)),
        preferred_element_type=F32,
    )
    row_slot = (iota((256, 320), 0) % 16).astype(F32)
    left = jnp.where(row_slot == owner_lane, by_column, 0.0).astype(BF16)

    for v in range(3):
        loads[v].wait()
        for a in range(0, 20, 4):
            pieces = [f_buf[v, :, a + q, :, :].reshape(320, 32) for q in range(4)]
            f_cat[:, pl.ds(v * 640 + a * 32, 128)] = jnp.concatenate(pieces, axis=1)

    other_table = pltpu.make_async_remote_copy(
        src_ref=table.at[other], dst_ref=t_nat.at[pl.ds(480, 480)], send_sem=t_sem.at[1], recv_sem=t_sem.at[2],
        device_id=partner, device_id_type=MESH)
    other_mask = pltpu.make_async_remote_copy(
        src_ref=m_buf.at[0], dst_ref=m_buf.at[1], send_sem=m_sem.at[0], recv_sem=m_sem.at[1],
        device_id=partner, device_id_type=MESH)
    own_table = pltpu.make_async_copy(table.at[core], t_nat.at[pl.ds(0, 480)], t_sem.at[0])
    spread[pl.ds(15, 128, stride=16), :] = jnp.zeros((128, 128), F32)
    my_place = y * 64 + tm * 8 + (z % 4) * 2 + core

    for half in range(2):
        for v in range(3):
            part = jnp.dot(left[half * 128:half * 128 + 128], f_cat[:, v * 640:v * 640 + 640], preferred_element_type=F32)
            for a in range(5):
                spread[pl.ds(v * 5 + a, 128, stride=16), :] = part[:, a * 128:a * 128 + 128]
        send1[pl.ds(half * 128, 128)] = spread[...].astype(BF16).reshape(128, 16, 128)
        if half == 0:
            pl.semaphore_wait(barrier, 66)
            for dy in range(1, 4):
                greet(ready, 0, dy, 0, core)
            other_mask.start()
            other_table.start()
            own_table.start()
        stay = send1.at[half * 128 + tm * 16 + slot], cols.at[my_place]

        @pl.when(core == half)
        def _():
            pltpu.make_async_copy(*stay, r1_sem.at[0]).start()

        @pl.when(core != half)
        def _():
            pltpu.make_async_remote_copy(
                *stay, send_sem=s1_sem, recv_sem=r1_sem.at[0], device_id=partner, device_id_type=MESH).start()

        for dy in range(4):
            if half == 0 and dy == 1:
                pl.semaphore_wait(ready, 3)

            @pl.loop(0 if dy else 1, 32)
            def _(s):
                to_slot, to_tm = shifted(x, y, z, s // 8, dy, s % 8)
                pltpu.make_async_remote_copy(
                    src_ref=send1.at[half * 128 + to_tm * 16 + to_slot], dst_ref=cols.at[my_place],
                    send_sem=s1_sem, recv_sem=r1_sem.at[dy],
                    device_id=(to_slot * 2 + half, to_tm), device_id_type=MESH).start()

    mine = iota((256, 16), 0) % 16 == iota((256, 16), 1)
    from_slot = jnp.sum(jnp.where(mine, owner[...].astype(F32), 0.0), axis=1, keepdims=True)
    row, column = iota((256, 256), 0), iota((256, 256), 1)
    order[...] = one_hot(((column // 16).astype(F32) == from_slot) & (column % 16 == row // 16))
    give_order = pltpu.make_async_copy(order, order_out, o_sem)
    give_order.start()

    own_table.wait()
    other_table.wait()
    other_mask.wait()
    keep = jnp.concatenate(
        [m_buf[0, pl.ds(core, 1), :], m_buf[1, pl.ds(core, 1), :]], axis=1).astype(F32)

    @pl.loop(0, 4)
    def _(g):
        base = pl.multiple_of(g * 128, 128)
        def target(q):
            return g * 32 + (q // 16) % 8 * 20 + q // 128
        ana = jnp.zeros((960, 512), F32)
        syn = jnp.zeros((512, 960), F32)
        for v in range(3):
            window = t_nat[:, pl.ds(pl.multiple_of(v * 640 + base, 128), 256)]
            q, w = iota((256, 512), 1), iota((256, 512), 0)
            r = q % 16 - v * 5
            hot = one_hot((w == target(q) + r * 4) & (r >= 0) & (r < 5))
            ana += jnp.dot(window, hot, preferred_element_type=F32)
            q, w = iota((512, 256), 0), iota((512, 256), 1)
            r = q % 16 - v * 5
            hot = one_hot((w == target(q) + r * 4) & (r >= 0) & (r < 5))
            syn += lax.dot_general(hot, window, (((1,), (1,)), ((), ())), preferred_element_type=F32)
        part = pl.ds(pl.multiple_of(g * 512, 512), 512)
        t_syn[part, :] = (syn * keep).astype(BF16)
        t_ana[:, part] = ana.astype(BF16)

    for dy in range(4):
        g = (y + 4 - dy) % 4
        landed = cols.at[pl.ds(g * 64, 64)]
        pltpu.make_async_copy(landed, landed, r1_sem.at[dy]).wait()
        for a in range(4):
            pieces = [cols[pl.ds(g * 64 + t * 8, 8), :, a * 32:a * 32 + 32].reshape(128, 32) for t in range(8)]
            xmat[a * 128:a * 128 + 128, :] = jnp.concatenate(pieces, axis=1)
        add = jnp.dot(t_ana[:, pl.ds(pl.multiple_of(g * 512, 512), 512)], xmat[...], preferred_element_type=F32)
        if dy == 0:
            coef[...] = add
        elif dy < 3:
            coef[...] += add
        else:
            kept[...] = (coef[...] + add).astype(BF16)

    for dy in range(4):
        g = (y + dy) % 4
        back = jnp.dot(t_syn[pl.ds(pl.multiple_of(g * 512, 512), 512), :], kept[...], preferred_element_type=F32).astype(BF16)
        for t in range(8):
            pieces = [back[a * 128:a * 128 + 128, t * 32:t * 32 + 32] for a in range(4)]
            send2[pl.ds(g * 64 + t * 8, 8)] = jnp.concatenate(pieces, axis=1).reshape(8, 16, 128)
        home = arrived.at[core * 128 + tm * 16 + slot]
        if dy == 0:
            pltpu.make_async_copy(send2.at[my_place], home, r2_sem).start()
            pltpu.make_async_remote_copy(
                send2.at[y * 64 + tm * 8 + (z % 4) * 2 + other], home,
                send_sem=s2_sem, recv_sem=r2_sem, device_id=partner, device_id_type=MESH).start()

        @pl.loop(0 if dy else 1, 32)
        def _(s):
            to_slot, to_tm = shifted(x, y, z, s // 8, dy, s % 8)
            for to_core in range(2):
                pltpu.make_async_remote_copy(
                    src_ref=send2.at[g * 64 + to_tm * 8 + to_slot % 4 * 2 + to_core], dst_ref=home,
                    send_sem=s2_sem, recv_sem=r2_sem,
                    device_id=(to_slot * 2 + to_core, to_tm), device_id_type=MESH).start()

    give_order.wait()
    sent = pl.ds(0, 255)
    pltpu.make_async_copy(send1.at[sent], send1.at[sent], s1_sem).wait()
    pltpu.make_async_copy(send2.at[sent], send2.at[sent], s2_sem).wait()
    pltpu.make_async_copy(arrived, arrived, r2_sem).wait()


def exchange(fields, vmodes, owner, table, mask):
    vmem, hbm = pl.BlockSpec(memory_space=pltpu.VMEM), pl.BlockSpec(memory_space=pl.ANY)
    dma = pltpu.SemaphoreType.DMA
    return pl.pallas_call(
        exchange_kernel,
        out_shape=[jax.ShapeDtypeStruct((256, 16, 128), BF16), jax.ShapeDtypeStruct((256, 256), BF16)],
        in_specs=[hbm, vmem, vmem, hbm, vmem],
        out_specs=[hbm, hbm],
        scratch_shapes=[
            pltpu.VMEM((256, 256), BF16),
            pltpu.VMEM((3, 20, 20, 16, 32), BF16),
            pltpu.VMEM((320, 1920), BF16),
            pltpu.VMEM((2048, 128), F32),
            pltpu.VMEM((256, 16, 128), BF16),
            pltpu.VMEM((256, 16, 128), BF16),
            pltpu.VMEM((512, 256), BF16),
            pltpu.VMEM((960, 1920), BF16),
            pltpu.VMEM((960, 2048), BF16),
            pltpu.VMEM((2048, 960), BF16),
            pltpu.VMEM((2, 2, 480), jnp.int32),
            pltpu.VMEM((960, 256), F32),
            pltpu.VMEM((960, 256), BF16),
            pltpu.VMEM((256, 16, 128), BF16),
            dma, dma((3,)), dma((3,)), dma((2,)), dma, dma((4,)), dma, dma,
            pltpu.SemaphoreType.REGULAR,
        ],
        compiler_params=pltpu.CompilerParams(collective_id=0, has_side_effects=True, vmem_limit_bytes=50 * 2**20),
        name="exchange",
    )(fields, vmodes, owner, table, mask)


def layout_kernel(order, arrived, out, laid, sem):
    copies = []
    for t in range(8):
        tiles = [arrived[core, t].reshape(256, 128) for core in range(2)]
        rows = jnp.dot(order[...], jnp.concatenate(tiles, axis=1), preferred_element_type=F32)
        for core in range(2):
            for a in range(4):
                part = rows[:, core * 128:core * 128 + 128]
                part = (pltpu.roll(part, 128 - a * 32, 1) if a else part).astype(BF16)
                for r in range(15):
                    laid[t * 2 + core, r // 5, r % 5 * 4 + a] = part[r * 16:r * 16 + 16, 0:32]
        span = pl.ds(t * 2, 2)
        copies.append(pltpu.make_async_copy(laid.at[span], out.at[span], sem.at[t]))
        copies[-1].start()
    for copy in copies:
        copy.wait()


def lay_out(order, arrived):
    vmem = pl.BlockSpec(memory_space=pltpu.VMEM)
    return pl.pallas_call(
        layout_kernel,
        out_shape=jax.ShapeDtypeStruct((16, 3, 20, 16, 32), BF16),
        in_specs=[vmem, vmem],
        out_specs=pl.BlockSpec(memory_space=pl.ANY),
        scratch_shapes=[pltpu.VMEM((16, 3, 20, 16, 32), BF16), pltpu.SemaphoreType.DMA((8,))],
        compiler_params=pltpu.CompilerParams(vmem_limit_bytes=16 * 2**20),
        name="lay_out",
    )(order, arrived.reshape(2, 8, 16, 16, 128))


def body(fields, vmodes, owner_map, hough_table, keep_mask):
    arrived, order = exchange(fields, vmodes.T, owner_map.reshape(1, 16), hough_table, keep_mask)
    return lay_out(order, arrived)


def solution(mesh):
    in_specs = (P(None, None, "lat", None, "tm"), P(), P(), P("tm", "lat", None), P("tm", "lat"))
    out_specs = P(None, None, "lat", None, "tm")
    return jax.shard_map(body, mesh=mesh, in_specs=in_specs, out_specs=out_specs, check_vma=False)
```

```python
import functools

import jax
import jax.numpy as jnp
from jax import lax
from jax.experimental import pallas as pl
from jax.experimental.pallas import tpu as pltpu
from jax.sharding import PartitionSpec as P

MESH = pl.DeviceIdType.MESH
F32 = jnp.float32
BF16 = jnp.bfloat16


def iota(shape, dim):
    return lax.broadcasted_iota(jnp.int32, shape, dim)


def one_hot(cond):
    return jnp.where(cond, 1.0, 0.0).astype(BF16)


def position():
    lat, tm = lax.axis_index("lat"), lax.axis_index("tm")
    core, z_lo, y = lat % 2, (lat // 2) % 4, lat // 8
    x, z_hi = tm // 2, tm % 2
    return x, y, z_hi * 4 + z_lo, core


def shifted(x, y, z, dx, dy, dz):
    x, y, z = (x + dx) % 4, (y + dy) % 4, (z + dz) % 8
    return y * 4 + z % 4, x * 2 + z // 4


def exchange_kernel(
    fields, vmodes, owner, table, mask,
    arrived, order_out,
    v_buf, o_buf, order, f_buf, f_cat, spread, send1, cols, xmat, t_nat, t_ana, t_syn, m_buf, coef, kept, send2,
    i_sem, f_sem, t_sem, m_sem, s1_sem, r1_sem, s2_sem, r2_sem, ready,
):
    x, y, z, core = position()
    slot, tm = y * 4 + z % 4, x * 2 + z // 4
    lat = slot * 2 + core
    other = 1 - core
    partner = (slot * 2 + other, tm)

    barrier = pltpu.get_barrier_semaphore()

    def greet(sem, dx, dy, dz, to_core):
        s, t = shifted(x, y, z, dx, dy, dz)
        pl.semaphore_signal(sem, inc=1, device_id=(s * 2 + to_core, t), device_id_type=MESH)

    loads = [pltpu.make_async_copy(fields.at[v], f_buf.at[v], f_sem.at[v]) for v in range(3)]
    small = [
        pltpu.make_async_copy(src, dst, i_sem.at[i])
        for i, (src, dst) in enumerate(((vmodes, v_buf), (owner, o_buf), (mask, m_buf.at[0])))
    ]
    for load in small + loads:
        load.start()
    for dy in range(1, 4):
        greet(barrier, 0, dy, 0, core)
    greet(barrier, 0, 0, 0, other)

    @pl.loop(1, 32)
    def _(s):
        greet(barrier, s // 8, 0, s % 8, other)
        greet(barrier, s // 8, 0, s % 8, core)

    for load in small:
        load.wait()

    row_k = (iota((256, 16), 0) % 128) // 16 * 2 + iota((256, 16), 0) // 128
    pick_k = one_hot(row_k == iota((256, 16), 1))
    by_level = jnp.dot(pick_k, v_buf[...], preferred_element_type=F32).astype(BF16)
    by_column = jnp.dot(by_level, one_hot(iota((20, 320), 1) // 16 == iota((20, 320), 0)), preferred_element_type=F32)
    owner_lane = jnp.dot(
        o_buf[...].astype(F32).astype(BF16),
        one_hot(iota((16, 320), 1) % 16 == iota((16, 320), 0)),
        preferred_element_type=F32,
    )
    row_slot = (iota((256, 320), 0) % 16).astype(F32)
    left = jnp.where(row_slot == owner_lane, by_column, 0.0).astype(BF16)

    for v in range(3):
        loads[v].wait()
        for a in range(0, 20, 4):
            pieces = [f_buf[v, :, a + q, :, :].reshape(320, 32) for q in range(4)]
            f_cat[:, pl.ds(v * 640 + a * 32, 128)] = jnp.concatenate(pieces, axis=1)

    other_table = pltpu.make_async_remote_copy(
        src_ref=table.at[other], dst_ref=t_nat.at[pl.ds(480, 480)], send_sem=t_sem.at[1], recv_sem=t_sem.at[2],
        device_id=partner, device_id_type=MESH)
    other_mask = pltpu.make_async_remote_copy(
        src_ref=m_buf.at[0], dst_ref=m_buf.at[1], send_sem=m_sem.at[0], recv_sem=m_sem.at[1],
        device_id=partner, device_id_type=MESH)
    own_table = pltpu.make_async_copy(table.at[core], t_nat.at[pl.ds(0, 480)], t_sem.at[0])
    spread[pl.ds(15, 128, stride=16), :] = jnp.zeros((128, 128), F32)
    my_place = y * 64 + tm * 8 + (z % 4) * 2 + core

    for half in range(2):
        for v in range(3):
            part = jnp.dot(left[half * 128:half * 128 + 128], f_cat[:, v * 640:v * 640 + 640], preferred_element_type=F32)
            for a in range(5):
                spread[pl.ds(v * 5 + a, 128, stride=16), :] = part[:, a * 128:a * 128 + 128]
        send1[pl.ds(half * 128, 128)] = spread[...].astype(BF16).reshape(128, 16, 128)
        if half == 0:
            pl.semaphore_wait(barrier, 66)
            for dy in range(1, 4):
                greet(ready, 0, dy, 0, core)
            other_mask.start()
            other_table.start()
            own_table.start()
        stay = send1.at[half * 128 + tm * 16 + slot], cols.at[my_place]

        @pl.when(core == half)
        def _():
            pltpu.make_async_copy(*stay, r1_sem.at[0]).start()

        @pl.when(core != half)
        def _():
            pltpu.make_async_remote_copy(
                *stay, send_sem=s1_sem, recv_sem=r1_sem.at[0], device_id=partner, device_id_type=MESH).start()

        for dy in range(4):
            if half == 0 and dy == 1:
                pl.semaphore_wait(ready, 3)

            @pl.loop(0 if dy else 1, 32)
            def _(s):
                to_slot, to_tm = shifted(x, y, z, s // 8, dy, s % 8)
                pltpu.make_async_remote_copy(
                    src_ref=send1.at[half * 128 + to_tm * 16 + to_slot], dst_ref=cols.at[my_place],
                    send_sem=s1_sem, recv_sem=r1_sem.at[dy],
                    device_id=(to_slot * 2 + half, to_tm), device_id_type=MESH).start()

    mine = iota((256, 16), 0) % 16 == iota((256, 16), 1)
    from_slot = jnp.sum(jnp.where(mine, o_buf[...].astype(F32), 0.0), axis=1, keepdims=True)
    row, column = iota((256, 256), 0), iota((256, 256), 1)
    order[...] = one_hot(((column // 16).astype(F32) == from_slot) & (column % 16 == row // 16))
    give_order = pltpu.make_async_copy(order, order_out, i_sem.at[3])
    give_order.start()

    own_table.wait()
    other_table.wait()
    other_mask.wait()
    keep = jnp.concatenate(
        [m_buf[0, pl.ds(core, 1), :], m_buf[1, pl.ds(core, 1), :]], axis=1).astype(F32)

    @pl.loop(0, 4)
    def _(g):
        base = pl.multiple_of(g * 128, 128)
        def target(q):
            return g * 32 + (q // 16) % 8 * 20 + q // 128
        ana = jnp.zeros((960, 512), F32)
        syn = jnp.zeros((512, 960), F32)
        for v in range(3):
            window = t_nat[:, pl.ds(pl.multiple_of(v * 640 + base, 128), 256)]
            q, w = iota((256, 512), 1), iota((256, 512), 0)
            r = q % 16 - v * 5
            hot = one_hot((w == target(q) + r * 4) & (r >= 0) & (r < 5))
            ana += jnp.dot(window, hot, preferred_element_type=F32)
            q, w = iota((512, 256), 0), iota((512, 256), 1)
            r = q % 16 - v * 5
            hot = one_hot((w == target(q) + r * 4) & (r >= 0) & (r < 5))
            syn += lax.dot_general(hot, window, (((1,), (1,)), ((), ())), preferred_element_type=F32)
        part = pl.ds(pl.multiple_of(g * 512, 512), 512)
        t_syn[part, :] = (syn * keep).astype(BF16)
        t_ana[:, part] = ana.astype(BF16)

    for dy in range(4):
        g = (y + 4 - dy) % 4
        landed = cols.at[pl.ds(g * 64, 64)]
        pltpu.make_async_copy(landed, landed, r1_sem.at[dy]).wait()
        for a in range(4):
            pieces = [cols[pl.ds(g * 64 + t * 8, 8), :, a * 32:a * 32 + 32].reshape(128, 32) for t in range(8)]
            xmat[a * 128:a * 128 + 128, :] = jnp.concatenate(pieces, axis=1)
        add = jnp.dot(t_ana[:, pl.ds(pl.multiple_of(g * 512, 512), 512)], xmat[...], preferred_element_type=F32)
        if dy == 0:
            coef[...] = add
        elif dy < 3:
            coef[...] += add
        else:
            kept[...] = (coef[...] + add).astype(BF16)

    for dy in range(4):
        g = (y + dy) % 4
        back = jnp.dot(t_syn[pl.ds(pl.multiple_of(g * 512, 512), 512), :], kept[...], preferred_element_type=F32).astype(BF16)
        for t in range(8):
            pieces = [back[a * 128:a * 128 + 128, t * 32:t * 32 + 32] for a in range(4)]
            send2[pl.ds(g * 64 + t * 8, 8)] = jnp.concatenate(pieces, axis=1).reshape(8, 16, 128)
        home = arrived.at[core * 128 + tm * 16 + slot]
        if dy == 0:
            pltpu.make_async_copy(send2.at[my_place], home, r2_sem).start()
            pltpu.make_async_remote_copy(
                send2.at[y * 64 + tm * 8 + (z % 4) * 2 + other], home,
                send_sem=s2_sem, recv_sem=r2_sem, device_id=partner, device_id_type=MESH).start()

        @pl.loop(0 if dy else 1, 32)
        def _(s):
            to_slot, to_tm = shifted(x, y, z, s // 8, dy, s % 8)
            for to_core in range(2):
                pltpu.make_async_remote_copy(
                    src_ref=send2.at[g * 64 + to_tm * 8 + to_slot % 4 * 2 + to_core], dst_ref=home,
                    send_sem=s2_sem, recv_sem=r2_sem,
                    device_id=(to_slot * 2 + to_core, to_tm), device_id_type=MESH).start()

    give_order.wait()
    sent = pl.ds(0, 255)
    pltpu.make_async_copy(send1.at[sent], send1.at[sent], s1_sem).wait()
    pltpu.make_async_copy(send2.at[sent], send2.at[sent], s2_sem).wait()
    pltpu.make_async_copy(arrived, arrived, r2_sem).wait()


def exchange(fields, vmodes, owner, table, mask):
    hbm, free = pl.BlockSpec(memory_space=pltpu.HBM), pl.BlockSpec(memory_space=pl.ANY)
    dma = pltpu.SemaphoreType.DMA
    return pl.pallas_call(
        exchange_kernel,
        out_shape=[jax.ShapeDtypeStruct((256, 16, 128), BF16), jax.ShapeDtypeStruct((256, 256), BF16)],
        in_specs=[hbm] * 5,
        out_specs=[free, free],
        scratch_shapes=[
            pltpu.VMEM((16, 20), BF16),
            pltpu.VMEM((1, 16), jnp.int32),
            pltpu.VMEM((256, 256), BF16),
            pltpu.VMEM((3, 20, 20, 16, 32), BF16),
            pltpu.VMEM((320, 1920), BF16),
            pltpu.VMEM((2048, 128), F32),
            pltpu.VMEM((256, 16, 128), BF16),
            pltpu.VMEM((256, 16, 128), BF16),
            pltpu.VMEM((512, 256), BF16),
            pltpu.VMEM((960, 1920), BF16),
            pltpu.VMEM((960, 2048), BF16),
            pltpu.VMEM((2048, 960), BF16),
            pltpu.VMEM((2, 2, 480), jnp.int32),
            pltpu.VMEM((960, 256), F32),
            pltpu.VMEM((960, 256), BF16),
            pltpu.VMEM((256, 16, 128), BF16),
            dma((4,)), dma((3,)), dma((3,)), dma((2,)), dma, dma((4,)), dma, dma,
            pltpu.SemaphoreType.REGULAR,
        ],
        compiler_params=pltpu.CompilerParams(collective_id=0, has_side_effects=True, vmem_limit_bytes=50 * 2**20),
        name="exchange",
    )(*(pltpu.with_memory_space_constraint(ref, pltpu.HBM) for ref in (fields, vmodes, owner, table, mask)))


def layout_kernel(order, arrived, out, laid, sem):
    copies = []
    for t in range(8):
        tiles = [arrived[core, t].reshape(256, 128) for core in range(2)]
        rows = jnp.dot(order[...], jnp.concatenate(tiles, axis=1), preferred_element_type=F32)
        for core in range(2):
            for a in range(4):
                part = rows[:, core * 128:core * 128 + 128]
                part = (pltpu.roll(part, 128 - a * 32, 1) if a else part).astype(BF16)
                for r in range(15):
                    laid[t * 2 + core, r // 5, r % 5 * 4 + a] = part[r * 16:r * 16 + 16, 0:32]
        span = pl.ds(t * 2, 2)
        copies.append(pltpu.make_async_copy(laid.at[span], out.at[span], sem.at[t]))
        copies[-1].start()
    for copy in copies:
        copy.wait()


def lay_out(order, arrived):
    vmem = pl.BlockSpec(memory_space=pltpu.VMEM)
    return pl.pallas_call(
        layout_kernel,
        out_shape=jax.ShapeDtypeStruct((16, 3, 20, 16, 32), BF16),
        in_specs=[vmem, vmem],
        out_specs=pl.BlockSpec(memory_space=pl.ANY),
        scratch_shapes=[pltpu.VMEM((16, 3, 20, 16, 32), BF16), pltpu.SemaphoreType.DMA((8,))],
        compiler_params=pltpu.CompilerParams(vmem_limit_bytes=16 * 2**20),
        name="lay_out",
    )(order, arrived.reshape(2, 8, 16, 16, 128))


def body(fields, vmodes, owner_map, hough_table, keep_mask):
    arrived, order = exchange(fields, vmodes.T, owner_map.reshape(1, 16), hough_table, keep_mask)
    return lay_out(order, arrived)


def solution(mesh):
    in_specs = (P(None, None, "lat", None, "tm"), P(), P(), P("tm", "lat", None), P("tm", "lat"))
    out_specs = P(None, None, "lat", None, "tm")
    return jax.shard_map(body, mesh=mesh, in_specs=in_specs, out_specs=out_specs, check_vma=False)
```

```python
import functools

import jax
import jax.numpy as jnp
from jax import lax
from jax.experimental import pallas as pl
from jax.experimental.pallas import tpu as pltpu
from jax.sharding import PartitionSpec as P

MESH = pl.DeviceIdType.MESH
F32 = jnp.float32
BF16 = jnp.bfloat16


def iota(shape, dim):
    return lax.broadcasted_iota(jnp.int32, shape, dim)


def one_hot(cond):
    return jnp.where(cond, 1.0, 0.0).astype(BF16)


def position():
    lat, tm = lax.axis_index("lat"), lax.axis_index("tm")
    core, z_lo, y = lat % 2, (lat // 2) % 4, lat // 8
    x, z_hi = tm // 2, tm % 2
    return x, y, z_hi * 4 + z_lo, core


def shifted(x, y, z, dx, dy, dz):
    x, y, z = (x + dx) % 4, (y + dy) % 4, (z + dz) % 8
    return y * 4 + z % 4, x * 2 + z // 4


def exchange_kernel(
    fields, vmodes, owner, table, mask,
    arrived, order_out,
    v_buf, o_buf, order, f_buf, f_cat, spread, send1, cols, xmat, t_nat, t_ana, t_syn, m_buf, coef, kept, send2, handed,
    i_sem, f_sem, t_sem, m_sem, s1_sem, r1_sem, s2_sem, r2_sem, x_sem, h_sem, ready,
):
    x, y, z, core = position()
    slot, tm = y * 4 + z % 4, x * 2 + z // 4
    lat = slot * 2 + core
    other = 1 - core
    partner = (slot * 2 + other, tm)

    barrier = pltpu.get_barrier_semaphore()

    def greet(sem, dx, dy, dz, to_core):
        s, t = shifted(x, y, z, dx, dy, dz)
        pl.semaphore_signal(sem, inc=1, device_id=(s * 2 + to_core, t), device_id_type=MESH)

    loads = [pltpu.make_async_copy(fields.at[v], f_buf.at[v], f_sem.at[v]) for v in range(3)]
    small = [
        pltpu.make_async_copy(src, dst, i_sem.at[i])
        for i, (src, dst) in enumerate(((vmodes, v_buf), (owner, o_buf), (mask, m_buf.at[0])))
    ]
    for load in small + loads:
        load.start()
    for dy in range(1, 4):
        greet(barrier, 0, dy, 0, core)
    greet(barrier, 0, 0, 0, other)

    @pl.loop(1, 32)
    def _(s):
        greet(barrier, s // 8, 0, s % 8, other)
        greet(barrier, s // 8, 0, s % 8, core)

    for load in small:
        load.wait()

    row_k = (iota((256, 16), 0) % 128) // 16 * 2 + iota((256, 16), 0) // 128
    pick_k = one_hot(row_k == iota((256, 16), 1))
    by_level = jnp.dot(pick_k, v_buf[...], preferred_element_type=F32).astype(BF16)
    by_column = jnp.dot(by_level, one_hot(iota((20, 320), 1) // 16 == iota((20, 320), 0)), preferred_element_type=F32)
    owner_lane = jnp.dot(
        o_buf[...].astype(F32).astype(BF16),
        one_hot(iota((16, 320), 1) % 16 == iota((16, 320), 0)),
        preferred_element_type=F32,
    )
    row_slot = (iota((256, 320), 0) % 16).astype(F32)
    left = jnp.where(row_slot == owner_lane, by_column, 0.0).astype(BF16)

    for v in range(3):
        loads[v].wait()
        for a in range(0, 20, 4):
            pieces = [f_buf[v, :, a + q, :, :].reshape(320, 32) for q in range(4)]
            f_cat[:, pl.ds(v * 640 + a * 32, 128)] = jnp.concatenate(pieces, axis=1)

    other_table = pltpu.make_async_remote_copy(
        src_ref=table.at[other], dst_ref=t_nat.at[pl.ds(480, 480)], send_sem=t_sem.at[1], recv_sem=t_sem.at[2],
        device_id=partner, device_id_type=MESH)
    other_mask = pltpu.make_async_remote_copy(
        src_ref=m_buf.at[0], dst_ref=m_buf.at[1], send_sem=m_sem.at[0], recv_sem=m_sem.at[1],
        device_id=partner, device_id_type=MESH)
    own_table = pltpu.make_async_copy(table.at[core], t_nat.at[pl.ds(0, 480)], t_sem.at[0])
    my_place = y * 64 + tm * 8 + (z % 4) * 2 + core

    for half in range(2):
        if half == 0:
            spread[pl.ds(15, 128, stride=16), :] = jnp.dot(left[128:256], f_cat[:, 1792:1920], preferred_element_type=F32)
        for v in range(3):
            part = jnp.dot(left[half * 128:half * 128 + 128], f_cat[:, v * 640:v * 640 + 640], preferred_element_type=F32)
            for a in range(5):
                spread[pl.ds(v * 5 + a, 128, stride=16), :] = part[:, a * 128:a * 128 + 128]
        send1[pl.ds(half * 128, 128)] = spread[...].astype(BF16).reshape(128, 8, 2, 128)
        if half == 0:
            pl.semaphore_wait(barrier, 66)
            for dy in range(1, 4):
                greet(ready, 0, dy, 0, core)
            other_mask.start()
            other_table.start()
            own_table.start()
        pairs = pl.ds(0, 8 - half)
        stay = send1.at[half * 128 + tm * 16 + slot, pairs], cols.at[my_place, pairs]

        @pl.when(core == half)
        def _():
            pltpu.make_async_copy(*stay, r1_sem.at[0]).start()

        @pl.when(core != half)
        def _():
            pltpu.make_async_remote_copy(
                *stay, send_sem=s1_sem.at[half], recv_sem=r1_sem.at[0], device_id=partner, device_id_type=MESH).start()

        for dy in range(4):
            if half == 0 and dy == 1:
                pl.semaphore_wait(ready, 3)

            @pl.loop(0 if dy else 1, 32)
            def _(s):
                to_slot, to_tm = shifted(x, y, z, s // 8, dy, s % 8)
                pltpu.make_async_remote_copy(
                    src_ref=send1.at[half * 128 + to_tm * 16 + to_slot, pairs], dst_ref=cols.at[my_place, pairs],
                    send_sem=s1_sem.at[half], recv_sem=r1_sem.at[dy],
                    device_id=(to_slot * 2 + half, to_tm), device_id_type=MESH).start()

    mine = iota((256, 16), 0) % 16 == iota((256, 16), 1)
    from_slot = jnp.sum(jnp.where(mine, o_buf[...].astype(F32), 0.0), axis=1, keepdims=True)
    row, column = iota((256, 256), 0), iota((256, 256), 1)
    order[...] = one_hot(((column // 16).astype(F32) == from_slot) & (column % 16 == row // 16))
    give_order = pltpu.make_async_copy(order, order_out, i_sem.at[3])
    give_order.start()

    own_table.wait()
    other_table.wait()
    other_mask.wait()
    keep = jnp.concatenate(
        [m_buf[0, pl.ds(core, 1), :], m_buf[1, pl.ds(core, 1), :]], axis=1).astype(F32)

    @pl.loop(0, 4)
    def _(g):
        base = pl.multiple_of(g * 128, 128)
        def target(q):
            return g * 32 + (q // 16) % 8 * 20 + q // 128
        def row_of(q):
            return jnp.where(q % 16 < 14, q % 16, jnp.where(q % 16 == 14 + core, 14, -1))
        ana = jnp.zeros((960, 512), F32)
        syn = jnp.zeros((512, 960), F32)
        for v in range(3):
            window = t_nat[:, pl.ds(pl.multiple_of(v * 640 + base, 128), 256)]
            q, w = iota((256, 512), 1), iota((256, 512), 0)
            r = row_of(q) - v * 5
            hot = one_hot((w == target(q) + r * 4) & (r >= 0) & (r < 5))
            ana += jnp.dot(window, hot, preferred_element_type=F32)
            q, w = iota((512, 256), 0), iota((512, 256), 1)
            r = row_of(q) - v * 5
            hot = one_hot((w == target(q) + r * 4) & (r >= 0) & (r < 5))
            syn += lax.dot_general(hot, window, (((1,), (1,)), ((), ())), preferred_element_type=F32)
        part = pl.ds(pl.multiple_of(g * 512, 512), 512)
        t_syn[part, :] = (syn * keep).astype(BF16)
        t_ana[:, part] = ana.astype(BF16)

    for dy in range(4):
        g = (y + 4 - dy) % 4
        block = pl.ds(g * 64, 64)
        lent = pltpu.make_async_remote_copy(
            src_ref=cols.at[block, 7], dst_ref=cols.at[block, 7], send_sem=x_sem.at[dy], recv_sem=x_sem.at[4 + dy],
            device_id=partner, device_id_type=MESH)

        @pl.when(core == 0)
        def _():
            pltpu.make_async_copy(cols.at[block], cols.at[block], r1_sem.at[dy]).wait()
            lent.start()

        @pl.when(core == 1)
        def _():
            first = cols.at[block, pl.ds(0, 7)]
            pltpu.make_async_copy(first, first, r1_sem.at[dy]).wait()
            lent.wait_recv()

        tiles = [cols[pl.ds(g * 64 + t * 8, 8)].reshape(128, 128) for t in range(8)]
        for a in range(4):
            pieces = [tile[:, a * 32:a * 32 + 32] for tile in tiles]
            xmat[a * 128:a * 128 + 128, :] = jnp.concatenate(pieces, axis=1)
        add = jnp.dot(t_ana[:, pl.ds(pl.multiple_of(g * 512, 512), 512)], xmat[...], preferred_element_type=F32)
        if dy == 0:
            coef[...] = add
        elif dy < 3:
            coef[...] += add
        else:
            kept[...] = (coef[...] + add).astype(BF16)

    for dy in range(4):
        g = (y + dy) % 4
        back = jnp.dot(t_syn[pl.ds(pl.multiple_of(g * 512, 512), 512), :], kept[...], preferred_element_type=F32).astype(BF16)
        for t in range(8):
            pieces = [back[a * 128:a * 128 + 128, t * 32:t * 32 + 32] for a in range(4)]
            send2[pl.ds(g * 64 + t * 8, 8)] = jnp.concatenate(pieces, axis=1).reshape(8, 8, 2, 128)
        block = pl.ds(g * 64, 64)
        hand = pltpu.make_async_remote_copy(
            src_ref=send2.at[block, 7], dst_ref=handed.at[block], send_sem=h_sem.at[dy], recv_sem=h_sem.at[4 + dy],
            device_id=partner, device_id_type=MESH)

        def give_back(my_core):
            pairs = pl.ds(0, 7 + my_core)
            home = arrived.at[my_core * 128 + tm * 16 + slot, pairs]
            if dy == 0:
                pltpu.make_async_copy(send2.at[my_place, pairs], home, r2_sem.at[my_core]).start()
                pltpu.make_async_remote_copy(
                    send2.at[y * 64 + tm * 8 + (z % 4) * 2 + 1 - my_core, pairs], home,
                    send_sem=s2_sem, recv_sem=r2_sem.at[my_core], device_id=partner, device_id_type=MESH).start()

            @pl.loop(0 if dy else 1, 32)
            def _(s):
                to_slot, to_tm = shifted(x, y, z, s // 8, dy, s % 8)
                for to_core in range(2):
                    pltpu.make_async_remote_copy(
                        src_ref=send2.at[g * 64 + to_tm * 8 + to_slot % 4 * 2 + to_core, pairs], dst_ref=home,
                        send_sem=s2_sem, recv_sem=r2_sem.at[my_core],
                        device_id=(to_slot * 2 + to_core, to_tm), device_id_type=MESH).start()

        @pl.when(core == 0)
        def _():
            hand.start()
            give_back(0)

        @pl.when(core == 1)
        def _():
            hand.wait_recv()
            send2[block, 7] = send2[block, 7] + handed[block]
            give_back(1)

    give_order.wait()

    def settle(ref, sem):
        pltpu.make_async_copy(ref, ref, sem).wait()

    @pl.when(core == 0)
    def _():
        settle(send1.at[pl.ds(0, 127)], s1_sem.at[0])
        settle(send1.at[pl.ds(0, 128), pl.ds(0, 7)], s1_sem.at[1])
        settle(send2.at[pl.ds(0, 255), pl.ds(0, 7)], s2_sem)
        for dy in range(4):
            settle(handed.at[pl.ds(0, 64)], x_sem.at[dy])
            settle(handed.at[pl.ds(0, 64)], h_sem.at[dy])

    @pl.when(core == 1)
    def _():
        settle(send1.at[pl.ds(0, 128)], s1_sem.at[0])
        settle(send1.at[pl.ds(0, 127), pl.ds(0, 7)], s1_sem.at[1])
        settle(send2.at[pl.ds(0, 255)], s2_sem)

    settle(arrived.at[pl.ds(0, 128), pl.ds(0, 7)], r2_sem.at[0])
    settle(arrived.at[pl.ds(128, 128)], r2_sem.at[1])


def exchange(fields, vmodes, owner, table, mask):
    hbm, free = pl.BlockSpec(memory_space=pltpu.HBM), pl.BlockSpec(memory_space=pl.ANY)
    dma = pltpu.SemaphoreType.DMA
    return pl.pallas_call(
        exchange_kernel,
        out_shape=[jax.ShapeDtypeStruct((256, 8, 2, 128), BF16), jax.ShapeDtypeStruct((256, 256), BF16)],
        in_specs=[hbm] * 5,
        out_specs=[free, free],
        scratch_shapes=[
            pltpu.VMEM((16, 20), BF16),
            pltpu.VMEM((1, 16), jnp.int32),
            pltpu.VMEM((256, 256), BF16),
            pltpu.VMEM((3, 20, 20, 16, 32), BF16),
            pltpu.VMEM((320, 1920), BF16),
            pltpu.VMEM((2048, 128), F32),
            pltpu.VMEM((256, 8, 2, 128), BF16),
            pltpu.VMEM((256, 8, 2, 128), BF16),
            pltpu.VMEM((512, 256), BF16),
            pltpu.VMEM((960, 1920), BF16),
            pltpu.VMEM((960, 2048), BF16),
            pltpu.VMEM((2048, 960), BF16),
            pltpu.VMEM((2, 2, 480), jnp.int32),
            pltpu.VMEM((960, 256), F32),
            pltpu.VMEM((960, 256), BF16),
            pltpu.VMEM((256, 8, 2, 128), BF16),
            pltpu.VMEM((256, 2, 128), BF16),
            dma((4,)), dma((3,)), dma((3,)), dma((2,)), dma((2,)), dma((4,)), dma, dma((2,)), dma((8,)), dma((8,)),
            pltpu.SemaphoreType.REGULAR,
        ],
        compiler_params=pltpu.CompilerParams(collective_id=0, has_side_effects=True, vmem_limit_bytes=50 * 2**20),
        name="exchange",
    )(*(pltpu.with_memory_space_constraint(ref, pltpu.HBM) for ref in (fields, vmodes, owner, table, mask)))


def layout_kernel(order, arrived, out, laid, sem):
    copies = []
    for t in range(8):
        first = jnp.where(iota((256, 128), 0) % 16 < 14, arrived[0, t].reshape(256, 128).astype(F32), 0.0).astype(BF16)
        both = jnp.concatenate([first, arrived[1, t].reshape(256, 128)], axis=1)
        rows = jnp.dot(order[...], both, preferred_element_type=F32)
        for core in range(2):
            for a in range(4):
                part = rows[:, core * 128:core * 128 + 128]
                part = (pltpu.roll(part, 128 - a * 32, 1) if a else part).astype(BF16)
                for r in range(14):
                    laid[t * 2 + core, r // 5, r % 5 * 4 + a] = part[r * 16:r * 16 + 16, 0:32]
                if core == 1:
                    laid[t * 2, 2, 16 + a] = part[224:240, 0:32]
                    laid[t * 2 + 1, 2, 16 + a] = part[240:256, 0:32]
        span = pl.ds(t * 2, 2)
        copies.append(pltpu.make_async_copy(laid.at[span], out.at[span], sem.at[t]))
        copies[-1].start()
    for copy in copies:
        copy.wait()


def lay_out(order, arrived):
    vmem = pl.BlockSpec(memory_space=pltpu.VMEM)
    return pl.pallas_call(
        layout_kernel,
        out_shape=jax.ShapeDtypeStruct((16, 3, 20, 16, 32), BF16),
        in_specs=[vmem, vmem],
        out_specs=pl.BlockSpec(memory_space=pl.ANY),
        scratch_shapes=[pltpu.VMEM((16, 3, 20, 16, 32), BF16), pltpu.SemaphoreType.DMA((8,))],
        compiler_params=pltpu.CompilerParams(vmem_limit_bytes=16 * 2**20),
        name="lay_out",
    )(order, arrived.reshape(2, 8, 16, 16, 128))


def body(fields, vmodes, owner_map, hough_table, keep_mask):
    arrived, order = exchange(fields, vmodes.T, owner_map.reshape(1, 16), hough_table, keep_mask)
    return lay_out(order, arrived)


def solution(mesh):
    in_specs = (P(None, None, "lat", None, "tm"), P(), P(), P("tm", "lat", None), P("tm", "lat"))
    out_specs = P(None, None, "lat", None, "tm")
    return jax.shard_map(body, mesh=mesh, in_specs=in_specs, out_specs=out_specs, check_vma=False)
```

```python
import functools

import jax
import jax.numpy as jnp
from jax import lax
from jax.experimental import pallas as pl
from jax.experimental.pallas import tpu as pltpu
from jax.sharding import PartitionSpec as P

MESH = pl.DeviceIdType.MESH
F32 = jnp.float32
BF16 = jnp.bfloat16


def iota(shape, dim):
    return lax.broadcasted_iota(jnp.int32, shape, dim)


def one_hot(cond):
    return jnp.where(cond, 1.0, 0.0).astype(BF16)


def position():
    lat, tm = lax.axis_index("lat"), lax.axis_index("tm")
    core, z_lo, y = lat % 2, (lat // 2) % 4, lat // 8
    x, z_hi = tm // 2, tm % 2
    return x, y, z_hi * 4 + z_lo, core


def exchange_kernel(
    fields, vmodes, owner, table, mask,
    arrived, order_out,
    v_buf, o_buf, order, f_buf, f_cat, spread, send1, cols, xmat, t_nat, t_ana, t_syn, m_buf, coef, kept, send2, handed,
    i_sem, f_sem, t_sem, m_sem, s1_sem, r1_sem, s2_sem, r2_sem, x_sem, h_sem, ready,
):
    x, y, z, core = position()
    slot, tm = y * 4 + z % 4, x * 2 + z // 4
    by_x = [(x + dx) % 4 * 2 for dx in range(4)]
    by_y = [(y + dy) % 4 * 4 for dy in range(4)]
    by_z = [((z + dz) % 8 % 4, (z + dz) % 8 // 4) for dz in range(8)]

    def each_chip(dy, visit):
        if dy == 0:
            for low, high in by_z[1:]:
                visit(by_y[0] + low, by_x[0] + high)

        @pl.loop(0 if dy else 1, 4)
        def _(dx):
            along_x = (x + dx) % 4 * 2
            for low, high in by_z:
                visit(by_y[dy] + low, along_x + high)

    lat = slot * 2 + core
    other = 1 - core
    partner = (slot * 2 + other, tm)

    barrier = pltpu.get_barrier_semaphore()

    def greet(sem, to_slot, to_tm, to_core):
        pl.semaphore_signal(sem, inc=1, device_id=(to_slot * 2 + to_core, to_tm), device_id_type=MESH)

    loads = [pltpu.make_async_copy(fields.at[v], f_buf.at[v], f_sem.at[v]) for v in range(3)]
    small = [
        pltpu.make_async_copy(src, dst, i_sem.at[i])
        for i, (src, dst) in enumerate(((vmodes, v_buf), (owner, o_buf), (mask, m_buf.at[0])))
    ]
    for load in small + loads:
        load.start()
    for dx in range(4):
        for dz, (low, high) in enumerate(by_z):
            greet(barrier, by_y[0] + low, by_x[dx] + high, other)
            if dx or dz:
                greet(barrier, by_y[0] + low, by_x[dx] + high, core)
    for dy in range(1, 4):
        greet(barrier, by_y[dy] + by_z[0][0], tm, core)

    for load in small:
        load.wait()

    row_k = (iota((256, 16), 0) % 128) // 16 * 2 + iota((256, 16), 0) // 128
    pick_k = one_hot(row_k == iota((256, 16), 1))
    by_level = jnp.dot(pick_k, v_buf[...], preferred_element_type=F32).astype(BF16)
    by_column = jnp.dot(by_level, one_hot(iota((20, 320), 1) // 16 == iota((20, 320), 0)), preferred_element_type=F32)
    owner_lane = jnp.dot(
        o_buf[...].astype(F32).astype(BF16),
        one_hot(iota((16, 320), 1) % 16 == iota((16, 320), 0)),
        preferred_element_type=F32,
    )
    row_slot = (iota((256, 320), 0) % 16).astype(F32)
    left = jnp.where(row_slot == owner_lane, by_column, 0.0).astype(BF16)

    for v in range(3):
        loads[v].wait()
        for a in range(0, 20, 4):
            pieces = [f_buf[v, :, a + q, :, :].reshape(320, 32) for q in range(4)]
            f_cat[:, pl.ds(v * 640 + a * 32, 128)] = jnp.concatenate(pieces, axis=1)

    other_table = pltpu.make_async_remote_copy(
        src_ref=table.at[other], dst_ref=t_nat.at[pl.ds(480, 480)], send_sem=t_sem.at[1], recv_sem=t_sem.at[2],
        device_id=partner, device_id_type=MESH)
    other_mask = pltpu.make_async_remote_copy(
        src_ref=m_buf.at[0], dst_ref=m_buf.at[1], send_sem=m_sem.at[0], recv_sem=m_sem.at[1],
        device_id=partner, device_id_type=MESH)
    own_table = pltpu.make_async_copy(table.at[core], t_nat.at[pl.ds(0, 480)], t_sem.at[0])
    my_place = y * 64 + tm * 8 + (z % 4) * 2 + core

    for half in range(2):
        if half == 0:
            spread[pl.ds(15, 128, stride=16), :] = jnp.dot(left[128:256], f_cat[:, 1792:1920], preferred_element_type=F32)
        for v in range(3):
            part = jnp.dot(left[half * 128:half * 128 + 128], f_cat[:, v * 640:v * 640 + 640], preferred_element_type=F32)
            for a in range(5):
                spread[pl.ds(v * 5 + a, 128, stride=16), :] = part[:, a * 128:a * 128 + 128]
        send1[pl.ds(half * 128, 128)] = spread[...].astype(BF16).reshape(128, 8, 2, 128)
        if half == 0:
            pl.semaphore_wait(barrier, 66)
            for dy in range(1, 4):
                greet(ready, by_y[dy] + by_z[0][0], tm, core)
            other_mask.start()
            other_table.start()
            own_table.start()
        pairs = pl.ds(0, 8 - half)
        stay = send1.at[half * 128 + tm * 16 + slot, pairs], cols.at[my_place, pairs]

        @pl.when(core == half)
        def _():
            pltpu.make_async_copy(*stay, r1_sem.at[0]).start()

        @pl.when(core != half)
        def _():
            pltpu.make_async_remote_copy(
                *stay, send_sem=s1_sem.at[half], recv_sem=r1_sem.at[0], device_id=partner, device_id_type=MESH).start()

        for dy in range(4):
            if half == 0 and dy == 1:
                pl.semaphore_wait(ready, 3)

            def send(to_slot, to_tm):
                pltpu.make_async_remote_copy(
                    src_ref=send1.at[half * 128 + to_tm * 16 + to_slot, pairs], dst_ref=cols.at[my_place, pairs],
                    send_sem=s1_sem.at[half], recv_sem=r1_sem.at[dy],
                    device_id=(to_slot * 2 + half, to_tm), device_id_type=MESH).start()

            each_chip(dy, send)

    mine = iota((256, 16), 0) % 16 == iota((256, 16), 1)
    from_slot = jnp.sum(jnp.where(mine, o_buf[...].astype(F32), 0.0), axis=1, keepdims=True)
    row, column = iota((256, 256), 0), iota((256, 256), 1)
    order[...] = one_hot(((column // 16).astype(F32) == from_slot) & (column % 16 == row // 16))
    give_order = pltpu.make_async_copy(order, order_out, i_sem.at[3])
    give_order.start()

    own_table.wait()
    other_table.wait()
    other_mask.wait()
    keep = jnp.concatenate(
        [m_buf[0, pl.ds(core, 1), :], m_buf[1, pl.ds(core, 1), :]], axis=1).astype(F32)

    @pl.loop(0, 4)
    def _(g):
        base = pl.multiple_of(g * 128, 128)
        def target(q):
            return g * 32 + (q // 16) % 8 * 20 + q // 128
        def row_of(q):
            return jnp.where(q % 16 < 14, q % 16, jnp.where(q % 16 == 14 + core, 14, -1))
        ana = jnp.zeros((960, 512), F32)
        syn = jnp.zeros((512, 960), F32)
        for v in range(3):
            window = t_nat[:, pl.ds(pl.multiple_of(v * 640 + base, 128), 256)]
            q, w = iota((256, 512), 1), iota((256, 512), 0)
            r = row_of(q) - v * 5
            hot = one_hot((w == target(q) + r * 4) & (r >= 0) & (r < 5))
            ana += jnp.dot(window, hot, preferred_element_type=F32)
            q, w = iota((512, 256), 0), iota((512, 256), 1)
            r = row_of(q) - v * 5
            hot = one_hot((w == target(q) + r * 4) & (r >= 0) & (r < 5))
            syn += lax.dot_general(hot, window, (((1,), (1,)), ((), ())), preferred_element_type=F32)
        part = pl.ds(pl.multiple_of(g * 512, 512), 512)
        t_syn[part, :] = (syn * keep).astype(BF16)
        t_ana[:, part] = ana.astype(BF16)

    for dy in range(4):
        g = (y + 4 - dy) % 4
        block = pl.ds(g * 64, 64)
        lent = pltpu.make_async_remote_copy(
            src_ref=cols.at[block, 7], dst_ref=cols.at[block, 7], send_sem=x_sem.at[dy], recv_sem=x_sem.at[4 + dy],
            device_id=partner, device_id_type=MESH)

        @pl.when(core == 0)
        def _():
            pltpu.make_async_copy(cols.at[block], cols.at[block], r1_sem.at[dy]).wait()
            lent.start()

        @pl.when(core == 1)
        def _():
            first = cols.at[block, pl.ds(0, 7)]
            pltpu.make_async_copy(first, first, r1_sem.at[dy]).wait()
            lent.wait_recv()

        tiles = [cols[pl.ds(g * 64 + t * 8, 8)].reshape(128, 128) for t in range(8)]
        for a in range(4):
            pieces = [tile[:, a * 32:a * 32 + 32] for tile in tiles]
            xmat[a * 128:a * 128 + 128, :] = jnp.concatenate(pieces, axis=1)
        add = jnp.dot(t_ana[:, pl.ds(pl.multiple_of(g * 512, 512), 512)], xmat[...], preferred_element_type=F32)
        if dy == 0:
            coef[...] = add
        elif dy < 3:
            coef[...] += add
        else:
            kept[...] = (coef[...] + add).astype(BF16)

    for dy in range(4):
        g = (y + dy) % 4
        back = jnp.dot(t_syn[pl.ds(pl.multiple_of(g * 512, 512), 512), :], kept[...], preferred_element_type=F32).astype(BF16)
        for t in range(8):
            pieces = [back[a * 128:a * 128 + 128, t * 32:t * 32 + 32] for a in range(4)]
            send2[pl.ds(g * 64 + t * 8, 8)] = jnp.concatenate(pieces, axis=1).reshape(8, 8, 2, 128)
        block = pl.ds(g * 64, 64)
        hand = pltpu.make_async_remote_copy(
            src_ref=send2.at[block, 7], dst_ref=handed.at[block], send_sem=h_sem.at[dy], recv_sem=h_sem.at[4 + dy],
            device_id=partner, device_id_type=MESH)

        def give_back(my_core):
            pairs = pl.ds(0, 7 + my_core)
            home = arrived.at[my_core * 128 + tm * 16 + slot, pairs]
            if dy == 0:
                pltpu.make_async_copy(send2.at[my_place, pairs], home, r2_sem.at[my_core]).start()
                pltpu.make_async_remote_copy(
                    send2.at[y * 64 + tm * 8 + (z % 4) * 2 + 1 - my_core, pairs], home,
                    send_sem=s2_sem, recv_sem=r2_sem.at[my_core], device_id=partner, device_id_type=MESH).start()

            def send(to_slot, to_tm):
                for to_core in range(2):
                    pltpu.make_async_remote_copy(
                        src_ref=send2.at[g * 64 + to_tm * 8 + to_slot % 4 * 2 + to_core, pairs], dst_ref=home,
                        send_sem=s2_sem, recv_sem=r2_sem.at[my_core],
                        device_id=(to_slot * 2 + to_core, to_tm), device_id_type=MESH).start()

            each_chip(dy, send)

        @pl.when(core == 0)
        def _():
            hand.start()
            give_back(0)

        @pl.when(core == 1)
        def _():
            hand.wait_recv()
            send2[block, 7] = send2[block, 7] + handed[block]
            give_back(1)

    give_order.wait()

    def settle(ref, sem):
        pltpu.make_async_copy(ref, ref, sem).wait()

    @pl.when(core == 0)
    def _():
        settle(send1.at[pl.ds(0, 127)], s1_sem.at[0])
        settle(send1.at[pl.ds(0, 128), pl.ds(0, 7)], s1_sem.at[1])
        settle(send2.at[pl.ds(0, 255), pl.ds(0, 7)], s2_sem)
        for dy in range(4):
            settle(handed.at[pl.ds(0, 64)], x_sem.at[dy])
            settle(handed.at[pl.ds(0, 64)], h_sem.at[dy])

    @pl.when(core == 1)
    def _():
        settle(send1.at[pl.ds(0, 128)], s1_sem.at[0])
        settle(send1.at[pl.ds(0, 127), pl.ds(0, 7)], s1_sem.at[1])
        settle(send2.at[pl.ds(0, 255)], s2_sem)

    settle(arrived.at[pl.ds(0, 128), pl.ds(0, 7)], r2_sem.at[0])
    settle(arrived.at[pl.ds(128, 128)], r2_sem.at[1])


def exchange(fields, vmodes, owner, table, mask):
    hbm, free = pl.BlockSpec(memory_space=pltpu.HBM), pl.BlockSpec(memory_space=pl.ANY)
    dma = pltpu.SemaphoreType.DMA
    return pl.pallas_call(
        exchange_kernel,
        out_shape=[jax.ShapeDtypeStruct((256, 8, 2, 128), BF16), jax.ShapeDtypeStruct((256, 256), BF16)],
        in_specs=[hbm] * 5,
        out_specs=[free, free],
        scratch_shapes=[
            pltpu.VMEM((16, 20), BF16),
            pltpu.VMEM((1, 16), jnp.int32),
            pltpu.VMEM((256, 256), BF16),
            pltpu.VMEM((3, 20, 20, 16, 32), BF16),
            pltpu.VMEM((320, 1920), BF16),
            pltpu.VMEM((2048, 128), F32),
            pltpu.VMEM((256, 8, 2, 128), BF16),
            pltpu.VMEM((256, 8, 2, 128), BF16),
            pltpu.VMEM((512, 256), BF16),
            pltpu.VMEM((960, 1920), BF16),
            pltpu.VMEM((960, 2048), BF16),
            pltpu.VMEM((2048, 960), BF16),
            pltpu.VMEM((2, 2, 480), jnp.int32),
            pltpu.VMEM((960, 256), F32),
            pltpu.VMEM((960, 256), BF16),
            pltpu.VMEM((256, 8, 2, 128), BF16),
            pltpu.VMEM((256, 2, 128), BF16),
            dma((4,)), dma((3,)), dma((3,)), dma((2,)), dma((2,)), dma((4,)), dma, dma((2,)), dma((8,)), dma((8,)),
            pltpu.SemaphoreType.REGULAR,
        ],
        compiler_params=pltpu.CompilerParams(collective_id=0, has_side_effects=True, vmem_limit_bytes=50 * 2**20),
        name="exchange",
    )(*(pltpu.with_memory_space_constraint(ref, pltpu.HBM) for ref in (fields, vmodes, owner, table, mask)))


def layout_kernel(order, arrived, out, laid, sem):
    copies = []
    for t in range(8):
        first = jnp.where(iota((256, 128), 0) % 16 < 14, arrived[0, t].reshape(256, 128).astype(F32), 0.0).astype(BF16)
        both = jnp.concatenate([first, arrived[1, t].reshape(256, 128)], axis=1)
        rows = jnp.dot(order[...], both, preferred_element_type=F32)
        for core in range(2):
            for a in range(4):
                part = rows[:, core * 128:core * 128 + 128]
                part = (pltpu.roll(part, 128 - a * 32, 1) if a else part).astype(BF16)
                for r in range(14):
                    laid[t * 2 + core, r // 5, r % 5 * 4 + a] = part[r * 16:r * 16 + 16, 0:32]
                if core == 1:
                    laid[t * 2, 2, 16 + a] = part[224:240, 0:32]
                    laid[t * 2 + 1, 2, 16 + a] = part[240:256, 0:32]
        span = pl.ds(t * 2, 2)
        copies.append(pltpu.make_async_copy(laid.at[span], out.at[span], sem.at[t]))
        copies[-1].start()
    for copy in copies:
        copy.wait()


def lay_out(order, arrived):
    vmem = pl.BlockSpec(memory_space=pltpu.VMEM)
    return pl.pallas_call(
        layout_kernel,
        out_shape=jax.ShapeDtypeStruct((16, 3, 20, 16, 32), BF16),
        in_specs=[vmem, vmem],
        out_specs=pl.BlockSpec(memory_space=pl.ANY),
        scratch_shapes=[pltpu.VMEM((16, 3, 20, 16, 32), BF16), pltpu.SemaphoreType.DMA((8,))],
        compiler_params=pltpu.CompilerParams(vmem_limit_bytes=16 * 2**20),
        name="lay_out",
    )(order, arrived.reshape(2, 8, 16, 16, 128))


def body(fields, vmodes, owner_map, hough_table, keep_mask):
    arrived, order = exchange(fields, vmodes.T, owner_map.reshape(1, 16), hough_table, keep_mask)
    return lay_out(order, arrived)


def solution(mesh):
    in_specs = (P(None, None, "lat", None, "tm"), P(), P(), P("tm", "lat", None), P("tm", "lat"))
    out_specs = P(None, None, "lat", None, "tm")
    return jax.shard_map(body, mesh=mesh, in_specs=in_specs, out_specs=out_specs, check_vma=False)
```

```python
import functools

import jax
import jax.numpy as jnp
from jax import lax
from jax.experimental import pallas as pl
from jax.experimental.pallas import tpu as pltpu
from jax.sharding import PartitionSpec as P

MESH = pl.DeviceIdType.MESH
F32 = jnp.float32
BF16 = jnp.bfloat16


def iota(shape, dim):
    return lax.broadcasted_iota(jnp.int32, shape, dim)


def one_hot(cond):
    return jnp.where(cond, 1.0, 0.0).astype(BF16)


def position():
    lat, tm = lax.axis_index("lat"), lax.axis_index("tm")
    core, z_lo, y = lat % 2, (lat // 2) % 4, lat // 8
    x, z_hi = tm // 2, tm % 2
    return x, y, z_hi * 4 + z_lo, core


def exchange_kernel(
    fields, vmodes, owner, table, mask,
    arrived, order_out,
    v_buf, o_buf, order, f_buf, f_cat, spread, send1, cols, xmat, t_nat, t_ana, t_syn, m_buf, coef, kept, send2, handed,
    i_sem, f_sem, t_sem, m_sem, s1_sem, r1_sem, s2_sem, r2_sem, x_sem, h_sem, ready,
):
    x, y, z, core = position()
    slot, tm = y * 4 + z % 4, x * 2 + z // 4
    by_x = [(x + dx) % 4 * 2 for dx in range(4)]
    by_y = [(y + dy) % 4 * 4 for dy in range(4)]
    by_z = [((z + dz) % 8 % 4, (z + dz) % 8 // 4) for dz in range(8)]

    def each_chip(dy, visit):
        if dy == 0:
            for low, high in by_z[1:]:
                visit(by_y[0] + low, by_x[0] + high)

        @pl.loop(0 if dy else 1, 4)
        def _(dx):
            along_x = (x + dx) % 4 * 2
            for low, high in by_z:
                visit(by_y[dy] + low, along_x + high)

    lat = slot * 2 + core
    other = 1 - core
    partner = (slot * 2 + other, tm)

    barrier = pltpu.get_barrier_semaphore()

    def greet(sem, to_slot, to_tm, to_core):
        pl.semaphore_signal(sem, inc=1, device_id=(to_slot * 2 + to_core, to_tm), device_id_type=MESH)

    loads = [pltpu.make_async_copy(fields.at[v], f_buf.at[v], f_sem.at[v]) for v in range(3)]
    small = [
        pltpu.make_async_copy(src, dst, i_sem.at[i])
        for i, (src, dst) in enumerate(((vmodes, v_buf), (owner, o_buf), (mask, m_buf.at[0])))
    ]
    for load in small + loads:
        load.start()
    for dx in range(4):
        for dz, (low, high) in enumerate(by_z):
            greet(barrier, by_y[0] + low, by_x[dx] + high, other)
            if dx or dz:
                greet(barrier, by_y[0] + low, by_x[dx] + high, core)
    for dy in range(1, 4):
        greet(barrier, by_y[dy] + by_z[0][0], tm, core)

    for load in small:
        load.wait()

    row_k = (iota((256, 16), 0) % 128) // 16 * 2 + iota((256, 16), 0) // 128
    pick_k = one_hot(row_k == iota((256, 16), 1))
    by_level = jnp.dot(pick_k, v_buf[...], preferred_element_type=F32).astype(BF16)
    by_column = jnp.dot(by_level, one_hot(iota((20, 320), 1) // 16 == iota((20, 320), 0)), preferred_element_type=F32)
    owner_lane = jnp.dot(
        o_buf[...].astype(F32).astype(BF16),
        one_hot(iota((16, 320), 1) % 16 == iota((16, 320), 0)),
        preferred_element_type=F32,
    )
    row_slot = (iota((256, 320), 0) % 16).astype(F32)
    left = jnp.where(row_slot == owner_lane, by_column, 0.0).astype(BF16)

    for v in range(3):
        loads[v].wait()
        for a in range(0, 20, 4):
            pieces = [f_buf[v, :, a + q, :, :].reshape(320, 32) for q in range(4)]
            f_cat[:, pl.ds(v * 640 + a * 32, 128)] = jnp.concatenate(pieces, axis=1)

    other_table = pltpu.make_async_remote_copy(
        src_ref=table.at[other], dst_ref=t_nat.at[pl.ds(480, 480)], send_sem=t_sem.at[1], recv_sem=t_sem.at[2],
        device_id=partner, device_id_type=MESH)
    other_mask = pltpu.make_async_remote_copy(
        src_ref=m_buf.at[0], dst_ref=m_buf.at[1], send_sem=m_sem.at[0], recv_sem=m_sem.at[1],
        device_id=partner, device_id_type=MESH)
    own_table = pltpu.make_async_copy(table.at[core], t_nat.at[pl.ds(0, 480)], t_sem.at[0])
    my_place = y * 64 + tm * 8 + (z % 4) * 2 + core

    for half in range(2):
        if half == 0:
            spread[pl.ds(15, 128, stride=16), :] = jnp.dot(left[128:256], f_cat[:, 1792:1920], preferred_element_type=F32)
        for v in range(3):
            part = jnp.dot(left[half * 128:half * 128 + 128], f_cat[:, v * 640:v * 640 + 640], preferred_element_type=F32)
            for a in range(5):
                spread[pl.ds(v * 5 + a, 128, stride=16), :] = part[:, a * 128:a * 128 + 128]
        send1[pl.ds(half * 128, 128)] = spread[...].astype(BF16).reshape(128, 8, 2, 128)
        if half == 0:
            pl.semaphore_wait(barrier, 66)
            for dy in range(1, 4):
                greet(ready, by_y[dy] + by_z[0][0], tm, core)
            other_mask.start()
            other_table.start()
            own_table.start()
        pairs = pl.ds(0, 8 - half)
        stay = send1.at[half * 128 + tm * 16 + slot, pairs], cols.at[my_place, pairs]

        @pl.when(core == half)
        def _():
            pltpu.make_async_copy(*stay, r1_sem.at[0]).start()

        @pl.when(core != half)
        def _():
            pltpu.make_async_remote_copy(
                *stay, send_sem=s1_sem.at[half], recv_sem=r1_sem.at[0], device_id=partner, device_id_type=MESH).start()

        for dy in range(4):
            if half == 0 and dy == 1:
                pl.semaphore_wait(ready, 3)

            def send(to_slot, to_tm):
                pltpu.make_async_remote_copy(
                    src_ref=send1.at[half * 128 + to_tm * 16 + to_slot, pairs], dst_ref=cols.at[my_place, pairs],
                    send_sem=s1_sem.at[half], recv_sem=r1_sem.at[dy],
                    device_id=(to_slot * 2 + half, to_tm), device_id_type=MESH).start()

            each_chip(dy, send)

    mine = iota((256, 16), 0) % 16 == iota((256, 16), 1)
    from_slot = jnp.sum(jnp.where(mine, o_buf[...].astype(F32), 0.0), axis=1, keepdims=True)
    row, column = iota((256, 256), 0), iota((256, 256), 1)
    order[...] = one_hot(((column // 16).astype(F32) == from_slot) & (column % 16 == row // 16))
    give_order = pltpu.make_async_copy(order, order_out, i_sem.at[3])
    give_order.start()

    own_table.wait()
    other_table.wait()
    other_mask.wait()
    keep = jnp.concatenate(
        [m_buf[0, pl.ds(core, 1), :], m_buf[1, pl.ds(core, 1), :]], axis=1).astype(F32)

    @pl.loop(0, 4)
    def _(g):
        base = pl.multiple_of(g * 128, 128)
        def target(q):
            return g * 32 + (q // 16) % 8 * 20 + q // 128
        def row_of(q):
            return jnp.where(q % 16 < 14, q % 16, jnp.where(q % 16 == 14 + core, 14, -1))
        ana = jnp.zeros((960, 512), F32)
        syn = jnp.zeros((512, 960), F32)
        for v in range(3):
            window = t_nat[:, pl.ds(pl.multiple_of(v * 640 + base, 128), 256)]
            q, w = iota((256, 512), 1), iota((256, 512), 0)
            r = row_of(q) - v * 5
            hot = one_hot((w == target(q) + r * 4) & (r >= 0) & (r < 5))
            ana += jnp.dot(window, hot, preferred_element_type=F32)
            q, w = iota((512, 256), 0), iota((512, 256), 1)
            r = row_of(q) - v * 5
            hot = one_hot((w == target(q) + r * 4) & (r >= 0) & (r < 5))
            syn += lax.dot_general(hot, window, (((1,), (1,)), ((), ())), preferred_element_type=F32)
        part = pl.ds(pl.multiple_of(g * 512, 512), 512)
        t_syn[part, :] = (syn * keep).astype(BF16)
        t_ana[:, part] = ana.astype(BF16)

    for dy in range(4):
        g = (y + 4 - dy) % 4
        block = pl.ds(g * 64, 64)
        lent = pltpu.make_async_remote_copy(
            src_ref=cols.at[block, 7], dst_ref=cols.at[block, 7], send_sem=x_sem.at[dy], recv_sem=x_sem.at[4 + dy],
            device_id=partner, device_id_type=MESH)

        @pl.when(core == 0)
        def _():
            pltpu.make_async_copy(cols.at[block], cols.at[block], r1_sem.at[dy]).wait()
            lent.start()

        @pl.when(core == 1)
        def _():
            first = cols.at[block, pl.ds(0, 7)]
            pltpu.make_async_copy(first, first, r1_sem.at[dy]).wait()
            lent.wait_recv()

        tiles = [cols[pl.ds(g * 64 + t * 8, 8)].reshape(128, 128) for t in range(8)]
        for a in range(4):
            pieces = [tile[:, a * 32:a * 32 + 32] for tile in tiles]
            xmat[a * 128:a * 128 + 128, :] = jnp.concatenate(pieces, axis=1)
        add = jnp.dot(t_ana[:, pl.ds(pl.multiple_of(g * 512, 512), 512)], xmat[...], preferred_element_type=F32)
        if dy == 0:
            coef[...] = add
        elif dy < 3:
            coef[...] += add
        else:
            kept[...] = (coef[...] + add).astype(BF16)

    for dy in (2, 1, 3, 0):
        g = (y + dy) % 4
        back = jnp.dot(t_syn[pl.ds(pl.multiple_of(g * 512, 512), 512), :], kept[...], preferred_element_type=F32).astype(BF16)
        for t in range(8):
            pieces = [back[a * 128:a * 128 + 128, t * 32:t * 32 + 32] for a in range(4)]
            send2[pl.ds(g * 64 + t * 8, 8)] = jnp.concatenate(pieces, axis=1).reshape(8, 8, 2, 128)
        block = pl.ds(g * 64, 64)
        hand = pltpu.make_async_remote_copy(
            src_ref=send2.at[block, 7], dst_ref=handed.at[block], send_sem=h_sem.at[dy], recv_sem=h_sem.at[4 + dy],
            device_id=partner, device_id_type=MESH)

        def give_back(my_core):
            pairs = pl.ds(0, 7 + my_core)
            home = arrived.at[my_core * 128 + tm * 16 + slot, pairs]
            if dy == 0:
                pltpu.make_async_copy(send2.at[my_place, pairs], home, r2_sem.at[my_core]).start()
                pltpu.make_async_remote_copy(
                    send2.at[y * 64 + tm * 8 + (z % 4) * 2 + 1 - my_core, pairs], home,
                    send_sem=s2_sem, recv_sem=r2_sem.at[my_core], device_id=partner, device_id_type=MESH).start()

            def send(to_slot, to_tm):
                for to_core in range(2):
                    pltpu.make_async_remote_copy(
                        src_ref=send2.at[g * 64 + to_tm * 8 + to_slot % 4 * 2 + to_core, pairs], dst_ref=home,
                        send_sem=s2_sem, recv_sem=r2_sem.at[my_core],
                        device_id=(to_slot * 2 + to_core, to_tm), device_id_type=MESH).start()

            each_chip(dy, send)

        @pl.when(core == 0)
        def _():
            hand.start()
            give_back(0)

        @pl.when(core == 1)
        def _():
            hand.wait_recv()
            send2[block, 7] = send2[block, 7] + handed[block]
            give_back(1)

    give_order.wait()

    def settle(ref, sem):
        pltpu.make_async_copy(ref, ref, sem).wait()

    @pl.when(core == 0)
    def _():
        settle(send1.at[pl.ds(0, 127)], s1_sem.at[0])
        settle(send1.at[pl.ds(0, 128), pl.ds(0, 7)], s1_sem.at[1])
        settle(send2.at[pl.ds(0, 255), pl.ds(0, 7)], s2_sem)
        for dy in range(4):
            settle(handed.at[pl.ds(0, 64)], x_sem.at[dy])
            settle(handed.at[pl.ds(0, 64)], h_sem.at[dy])

    @pl.when(core == 1)
    def _():
        settle(send1.at[pl.ds(0, 128)], s1_sem.at[0])
        settle(send1.at[pl.ds(0, 127), pl.ds(0, 7)], s1_sem.at[1])
        settle(send2.at[pl.ds(0, 255)], s2_sem)

    settle(arrived.at[pl.ds(0, 128), pl.ds(0, 7)], r2_sem.at[0])
    settle(arrived.at[pl.ds(128, 128)], r2_sem.at[1])


def exchange(fields, vmodes, owner, table, mask):
    hbm, free = pl.BlockSpec(memory_space=pltpu.HBM), pl.BlockSpec(memory_space=pl.ANY)
    dma = pltpu.SemaphoreType.DMA
    return pl.pallas_call(
        exchange_kernel,
        out_shape=[jax.ShapeDtypeStruct((256, 8, 2, 128), BF16), jax.ShapeDtypeStruct((256, 256), BF16)],
        in_specs=[hbm] * 5,
        out_specs=[free, free],
        scratch_shapes=[
            pltpu.VMEM((16, 20), BF16),
            pltpu.VMEM((1, 16), jnp.int32),
            pltpu.VMEM((256, 256), BF16),
            pltpu.VMEM((3, 20, 20, 16, 32), BF16),
            pltpu.VMEM((320, 1920), BF16),
            pltpu.VMEM((2048, 128), F32),
            pltpu.VMEM((256, 8, 2, 128), BF16),
            pltpu.VMEM((256, 8, 2, 128), BF16),
            pltpu.VMEM((512, 256), BF16),
            pltpu.VMEM((960, 1920), BF16),
            pltpu.VMEM((960, 2048), BF16),
            pltpu.VMEM((2048, 960), BF16),
            pltpu.VMEM((2, 2, 480), jnp.int32),
            pltpu.VMEM((960, 256), F32),
            pltpu.VMEM((960, 256), BF16),
            pltpu.VMEM((256, 8, 2, 128), BF16),
            pltpu.VMEM((256, 2, 128), BF16),
            dma((4,)), dma((3,)), dma((3,)), dma((2,)), dma((2,)), dma((4,)), dma, dma((2,)), dma((8,)), dma((8,)),
            pltpu.SemaphoreType.REGULAR,
        ],
        compiler_params=pltpu.CompilerParams(collective_id=0, has_side_effects=True, vmem_limit_bytes=50 * 2**20),
        name="exchange",
    )(*(pltpu.with_memory_space_constraint(ref, pltpu.HBM) for ref in (fields, vmodes, owner, table, mask)))


def layout_kernel(order, arrived, out, laid, sem):
    copies = []
    for t in range(8):
        first = jnp.where(iota((256, 128), 0) % 16 < 14, arrived[0, t].reshape(256, 128).astype(F32), 0.0).astype(BF16)
        both = jnp.concatenate([first, arrived[1, t].reshape(256, 128)], axis=1)
        rows = jnp.dot(order[...], both, preferred_element_type=F32)
        for core in range(2):
            for a in range(4):
                part = rows[:, core * 128:core * 128 + 128]
                part = (pltpu.roll(part, 128 - a * 32, 1) if a else part).astype(BF16)
                for r in range(14):
                    laid[t * 2 + core, r // 5, r % 5 * 4 + a] = part[r * 16:r * 16 + 16, 0:32]
                if core == 1:
                    laid[t * 2, 2, 16 + a] = part[224:240, 0:32]
                    laid[t * 2 + 1, 2, 16 + a] = part[240:256, 0:32]
        span = pl.ds(t * 2, 2)
        copies.append(pltpu.make_async_copy(laid.at[span], out.at[span], sem.at[t]))
        copies[-1].start()
    for copy in copies:
        copy.wait()


def lay_out(order, arrived):
    vmem = pl.BlockSpec(memory_space=pltpu.VMEM)
    return pl.pallas_call(
        layout_kernel,
        out_shape=jax.ShapeDtypeStruct((16, 3, 20, 16, 32), BF16),
        in_specs=[vmem, vmem],
        out_specs=pl.BlockSpec(memory_space=pl.ANY),
        scratch_shapes=[pltpu.VMEM((16, 3, 20, 16, 32), BF16), pltpu.SemaphoreType.DMA((8,))],
        compiler_params=pltpu.CompilerParams(vmem_limit_bytes=16 * 2**20),
        name="lay_out",
    )(order, arrived.reshape(2, 8, 16, 16, 128))


def body(fields, vmodes, owner_map, hough_table, keep_mask):
    arrived, order = exchange(fields, vmodes.T, owner_map.reshape(1, 16), hough_table, keep_mask)
    return lay_out(order, arrived)


def solution(mesh):
    in_specs = (P(None, None, "lat", None, "tm"), P(), P(), P("tm", "lat", None), P("tm", "lat"))
    out_specs = P(None, None, "lat", None, "tm")
    return jax.shard_map(body, mesh=mesh, in_specs=in_specs, out_specs=out_specs, check_vma=False)
```

```python
import functools

import jax
import jax.numpy as jnp
from jax import lax
from jax.experimental import pallas as pl
from jax.experimental.pallas import tpu as pltpu
from jax.sharding import PartitionSpec as P

MESH = pl.DeviceIdType.MESH
F32 = jnp.float32
BF16 = jnp.bfloat16


def iota(shape, dim):
    return lax.broadcasted_iota(jnp.int32, shape, dim)


def one_hot(cond):
    return jnp.where(cond, 1.0, 0.0).astype(BF16)


def position():
    lat, tm = lax.axis_index("lat"), lax.axis_index("tm")
    core, z_lo, y = lat % 2, (lat // 2) % 4, lat // 8
    x, z_hi = tm // 2, tm % 2
    return x, y, z_hi * 4 + z_lo, core


def exchange_kernel(
    fields, vmodes, owner, table, mask,
    arrived, order_out,
    v_buf, o_buf, order, f_buf, f_cat, spread, send1, cols, xmat, t_nat, t_ana, t_syn, m_buf, coef, kept, send2, handed,
    i_sem, f_sem, t_sem, m_sem, s1_sem, r1_sem, s2_sem, r2_sem, x_sem, h_sem, ready,
):
    x, y, z, core = position()
    slot, tm = y * 4 + z % 4, x * 2 + z // 4
    by_x = [(x + dx) % 4 * 2 for dx in range(4)]
    by_y = [(y + dy) % 4 * 4 for dy in range(4)]
    by_z = [((z + dz) % 8 % 4, (z + dz) % 8 // 4) for dz in range(8)]

    def each_chip(dy, visit):
        if dy == 0:
            for dz in (4, 3, 5, 2, 6, 1, 7):
                visit(by_y[0] + by_z[dz][0], by_x[0] + by_z[dz][1])

        @pl.loop(0 if dy else 1, 4)
        def _(dx):
            along_x = (x + dx) % 4 * 2
            for dz in (4, 3, 5, 2, 6, 1, 7, 0):
                visit(by_y[dy] + by_z[dz][0], along_x + by_z[dz][1])

    lat = slot * 2 + core
    other = 1 - core
    partner = (slot * 2 + other, tm)

    barrier = pltpu.get_barrier_semaphore()

    def greet(sem, to_slot, to_tm, to_core):
        pl.semaphore_signal(sem, inc=1, device_id=(to_slot * 2 + to_core, to_tm), device_id_type=MESH)

    loads = [pltpu.make_async_copy(fields.at[v], f_buf.at[v], f_sem.at[v]) for v in range(3)]
    small = [
        pltpu.make_async_copy(src, dst, i_sem.at[i])
        for i, (src, dst) in enumerate(((vmodes, v_buf), (owner, o_buf), (mask, m_buf.at[0])))
    ]
    for load in small + loads:
        load.start()
    for dx in range(4):
        for dz, (low, high) in enumerate(by_z):
            greet(barrier, by_y[0] + low, by_x[dx] + high, other)
            if dx or dz:
                greet(barrier, by_y[0] + low, by_x[dx] + high, core)
    for dy in range(1, 4):
        greet(barrier, by_y[dy] + by_z[0][0], tm, core)

    for load in small:
        load.wait()

    row_k = (iota((256, 16), 0) % 128) // 16 * 2 + iota((256, 16), 0) // 128
    pick_k = one_hot(row_k == iota((256, 16), 1))
    by_level = jnp.dot(pick_k, v_buf[...], preferred_element_type=F32).astype(BF16)
    by_column = jnp.dot(by_level, one_hot(iota((20, 320), 1) // 16 == iota((20, 320), 0)), preferred_element_type=F32)
    owner_lane = jnp.dot(
        o_buf[...].astype(F32).astype(BF16),
        one_hot(iota((16, 320), 1) % 16 == iota((16, 320), 0)),
        preferred_element_type=F32,
    )
    row_slot = (iota((256, 320), 0) % 16).astype(F32)
    left = jnp.where(row_slot == owner_lane, by_column, 0.0).astype(BF16)

    for v in range(3):
        loads[v].wait()
        for a in range(0, 20, 4):
            pieces = [f_buf[v, :, a + q, :, :].reshape(320, 32) for q in range(4)]
            f_cat[:, pl.ds(v * 640 + a * 32, 128)] = jnp.concatenate(pieces, axis=1)

    other_table = pltpu.make_async_remote_copy(
        src_ref=table.at[other], dst_ref=t_nat.at[pl.ds(480, 480)], send_sem=t_sem.at[1], recv_sem=t_sem.at[2],
        device_id=partner, device_id_type=MESH)
    other_mask = pltpu.make_async_remote_copy(
        src_ref=m_buf.at[0], dst_ref=m_buf.at[1], send_sem=m_sem.at[0], recv_sem=m_sem.at[1],
        device_id=partner, device_id_type=MESH)
    own_table = pltpu.make_async_copy(table.at[core], t_nat.at[pl.ds(0, 480)], t_sem.at[0])
    my_place = y * 64 + tm * 8 + (z % 4) * 2 + core

    for half in range(2):
        if half == 0:
            spread[pl.ds(15, 128, stride=16), :] = jnp.dot(left[128:256], f_cat[:, 1792:1920], preferred_element_type=F32)
        for v in range(3):
            part = jnp.dot(left[half * 128:half * 128 + 128], f_cat[:, v * 640:v * 640 + 640], preferred_element_type=F32)
            for a in range(5):
                spread[pl.ds(v * 5 + a, 128, stride=16), :] = part[:, a * 128:a * 128 + 128]
        send1[pl.ds(half * 128, 128)] = spread[...].astype(BF16).reshape(128, 8, 2, 128)
        if half == 0:
            pl.semaphore_wait(barrier, 66)
            for dy in range(1, 4):
                greet(ready, by_y[dy] + by_z[0][0], tm, core)
            other_mask.start()
            other_table.start()
            own_table.start()
        pairs = pl.ds(0, 8 - half)
        stay = send1.at[half * 128 + tm * 16 + slot, pairs], cols.at[my_place, pairs]

        @pl.when(core == half)
        def _():
            pltpu.make_async_copy(*stay, r1_sem.at[0]).start()

        @pl.when(core != half)
        def _():
            pltpu.make_async_remote_copy(
                *stay, send_sem=s1_sem.at[half], recv_sem=r1_sem.at[0], device_id=partner, device_id_type=MESH).start()

        for dy in range(4):
            if half == 0 and dy == 1:
                pl.semaphore_wait(ready, 3)

            def send(to_slot, to_tm):
                pltpu.make_async_remote_copy(
                    src_ref=send1.at[half * 128 + to_tm * 16 + to_slot, pairs], dst_ref=cols.at[my_place, pairs],
                    send_sem=s1_sem.at[half], recv_sem=r1_sem.at[dy],
                    device_id=(to_slot * 2 + half, to_tm), device_id_type=MESH).start()

            each_chip(dy, send)

    mine = iota((256, 16), 0) % 16 == iota((256, 16), 1)
    from_slot = jnp.sum(jnp.where(mine, o_buf[...].astype(F32), 0.0), axis=1, keepdims=True)
    row, column = iota((256, 256), 0), iota((256, 256), 1)
    order[...] = one_hot(((column // 16).astype(F32) == from_slot) & (column % 16 == row // 16))
    give_order = pltpu.make_async_copy(order, order_out, i_sem.at[3])
    give_order.start()

    own_table.wait()
    other_table.wait()
    other_mask.wait()
    keep = jnp.concatenate(
        [m_buf[0, pl.ds(core, 1), :], m_buf[1, pl.ds(core, 1), :]], axis=1).astype(F32)

    @pl.loop(0, 4)
    def _(g):
        base = pl.multiple_of(g * 128, 128)
        def target(q):
            return g * 32 + (q // 16) % 8 * 20 + q // 128
        def row_of(q):
            return jnp.where(q % 16 < 14, q % 16, jnp.where(q % 16 == 14 + core, 14, -1))
        ana = jnp.zeros((960, 512), F32)
        syn = jnp.zeros((512, 960), F32)
        for v in range(3):
            window = t_nat[:, pl.ds(pl.multiple_of(v * 640 + base, 128), 256)]
            q, w = iota((256, 512), 1), iota((256, 512), 0)
            r = row_of(q) - v * 5
            hot = one_hot((w == target(q) + r * 4) & (r >= 0) & (r < 5))
            ana += jnp.dot(window, hot, preferred_element_type=F32)
            q, w = iota((512, 256), 0), iota((512, 256), 1)
            r = row_of(q) - v * 5
            hot = one_hot((w == target(q) + r * 4) & (r >= 0) & (r < 5))
            syn += lax.dot_general(hot, window, (((1,), (1,)), ((), ())), preferred_element_type=F32)
        part = pl.ds(pl.multiple_of(g * 512, 512), 512)
        t_syn[part, :] = (syn * keep).astype(BF16)
        t_ana[:, part] = ana.astype(BF16)

    for dy in range(4):
        g = (y + 4 - dy) % 4
        block = pl.ds(g * 64, 64)
        lent = pltpu.make_async_remote_copy(
            src_ref=cols.at[block, 7], dst_ref=cols.at[block, 7], send_sem=x_sem.at[dy], recv_sem=x_sem.at[4 + dy],
            device_id=partner, device_id_type=MESH)

        @pl.when(core == 0)
        def _():
            pltpu.make_async_copy(cols.at[block], cols.at[block], r1_sem.at[dy]).wait()
            lent.start()

        @pl.when(core == 1)
        def _():
            first = cols.at[block, pl.ds(0, 7)]
            pltpu.make_async_copy(first, first, r1_sem.at[dy]).wait()
            lent.wait_recv()

        tiles = [cols[pl.ds(g * 64 + t * 8, 8)].reshape(128, 128) for t in range(8)]
        for a in range(4):
            pieces = [tile[:, a * 32:a * 32 + 32] for tile in tiles]
            xmat[a * 128:a * 128 + 128, :] = jnp.concatenate(pieces, axis=1)
        add = jnp.dot(t_ana[:, pl.ds(pl.multiple_of(g * 512, 512), 512)], xmat[...], preferred_element_type=F32)
        if dy == 0:
            coef[...] = add
        elif dy < 3:
            coef[...] += add
        else:
            kept[...] = (coef[...] + add).astype(BF16)

    for dy in (2, 1, 3, 0):
        g = (y + dy) % 4
        back = jnp.dot(t_syn[pl.ds(pl.multiple_of(g * 512, 512), 512), :], kept[...], preferred_element_type=F32).astype(BF16)
        for t in range(8):
            pieces = [back[a * 128:a * 128 + 128, t * 32:t * 32 + 32] for a in range(4)]
            send2[pl.ds(g * 64 + t * 8, 8)] = jnp.concatenate(pieces, axis=1).reshape(8, 8, 2, 128)
        block = pl.ds(g * 64, 64)
        hand = pltpu.make_async_remote_copy(
            src_ref=send2.at[block, 7], dst_ref=handed.at[block], send_sem=h_sem.at[dy], recv_sem=h_sem.at[4 + dy],
            device_id=partner, device_id_type=MESH)

        def give_back(my_core):
            pairs = pl.ds(0, 7 + my_core)
            home = arrived.at[my_core * 128 + tm * 16 + slot, pairs]
            if dy == 0:
                pltpu.make_async_copy(send2.at[my_place, pairs], home, r2_sem.at[my_core]).start()
                pltpu.make_async_remote_copy(
                    send2.at[y * 64 + tm * 8 + (z % 4) * 2 + 1 - my_core, pairs], home,
                    send_sem=s2_sem, recv_sem=r2_sem.at[my_core], device_id=partner, device_id_type=MESH).start()

            def send(to_slot, to_tm):
                for to_core in range(2):
                    pltpu.make_async_remote_copy(
                        src_ref=send2.at[g * 64 + to_tm * 8 + to_slot % 4 * 2 + to_core, pairs], dst_ref=home,
                        send_sem=s2_sem, recv_sem=r2_sem.at[my_core],
                        device_id=(to_slot * 2 + to_core, to_tm), device_id_type=MESH).start()

            each_chip(dy, send)

        @pl.when(core == 0)
        def _():
            hand.start()
            give_back(0)

        @pl.when(core == 1)
        def _():
            hand.wait_recv()
            send2[block, 7] = send2[block, 7] + handed[block]
            give_back(1)

    give_order.wait()

    def settle(ref, sem):
        pltpu.make_async_copy(ref, ref, sem).wait()

    @pl.when(core == 0)
    def _():
        settle(send1.at[pl.ds(0, 127)], s1_sem.at[0])
        settle(send1.at[pl.ds(0, 128), pl.ds(0, 7)], s1_sem.at[1])
        settle(send2.at[pl.ds(0, 255), pl.ds(0, 7)], s2_sem)
        for dy in range(4):
            settle(handed.at[pl.ds(0, 64)], x_sem.at[dy])
            settle(handed.at[pl.ds(0, 64)], h_sem.at[dy])

    @pl.when(core == 1)
    def _():
        settle(send1.at[pl.ds(0, 128)], s1_sem.at[0])
        settle(send1.at[pl.ds(0, 127), pl.ds(0, 7)], s1_sem.at[1])
        settle(send2.at[pl.ds(0, 255)], s2_sem)

    settle(arrived.at[pl.ds(0, 128), pl.ds(0, 7)], r2_sem.at[0])
    settle(arrived.at[pl.ds(128, 128)], r2_sem.at[1])


def exchange(fields, vmodes, owner, table, mask):
    hbm, free = pl.BlockSpec(memory_space=pltpu.HBM), pl.BlockSpec(memory_space=pl.ANY)
    dma = pltpu.SemaphoreType.DMA
    return pl.pallas_call(
        exchange_kernel,
        out_shape=[jax.ShapeDtypeStruct((256, 8, 2, 128), BF16), jax.ShapeDtypeStruct((256, 256), BF16)],
        in_specs=[hbm] * 5,
        out_specs=[free, free],
        scratch_shapes=[
            pltpu.VMEM((16, 20), BF16),
            pltpu.VMEM((1, 16), jnp.int32),
            pltpu.VMEM((256, 256), BF16),
            pltpu.VMEM((3, 20, 20, 16, 32), BF16),
            pltpu.VMEM((320, 1920), BF16),
            pltpu.VMEM((2048, 128), F32),
            pltpu.VMEM((256, 8, 2, 128), BF16),
            pltpu.VMEM((256, 8, 2, 128), BF16),
            pltpu.VMEM((512, 256), BF16),
            pltpu.VMEM((960, 1920), BF16),
            pltpu.VMEM((960, 2048), BF16),
            pltpu.VMEM((2048, 960), BF16),
            pltpu.VMEM((2, 2, 480), jnp.int32),
            pltpu.VMEM((960, 256), F32),
            pltpu.VMEM((960, 256), BF16),
            pltpu.VMEM((256, 8, 2, 128), BF16),
            pltpu.VMEM((256, 2, 128), BF16),
            dma((4,)), dma((3,)), dma((3,)), dma((2,)), dma((2,)), dma((4,)), dma, dma((2,)), dma((8,)), dma((8,)),
            pltpu.SemaphoreType.REGULAR,
        ],
        compiler_params=pltpu.CompilerParams(collective_id=0, has_side_effects=True, vmem_limit_bytes=50 * 2**20),
        name="exchange",
    )(*(pltpu.with_memory_space_constraint(ref, pltpu.HBM) for ref in (fields, vmodes, owner, table, mask)))


def layout_kernel(order, arrived, out, laid, sem):
    copies = []
    for t in range(8):
        first = jnp.where(iota((256, 128), 0) % 16 < 14, arrived[0, t].reshape(256, 128).astype(F32), 0.0).astype(BF16)
        both = jnp.concatenate([first, arrived[1, t].reshape(256, 128)], axis=1)
        rows = jnp.dot(order[...], both, preferred_element_type=F32)
        for core in range(2):
            for a in range(4):
                part = rows[:, core * 128:core * 128 + 128]
                part = (pltpu.roll(part, 128 - a * 32, 1) if a else part).astype(BF16)
                for r in range(14):
                    laid[t * 2 + core, r // 5, r % 5 * 4 + a] = part[r * 16:r * 16 + 16, 0:32]
                if core == 1:
                    laid[t * 2, 2, 16 + a] = part[224:240, 0:32]
                    laid[t * 2 + 1, 2, 16 + a] = part[240:256, 0:32]
        span = pl.ds(t * 2, 2)
        copies.append(pltpu.make_async_copy(laid.at[span], out.at[span], sem.at[t]))
        copies[-1].start()
    for copy in copies:
        copy.wait()


def lay_out(order, arrived):
    vmem = pl.BlockSpec(memory_space=pltpu.VMEM)
    return pl.pallas_call(
        layout_kernel,
        out_shape=jax.ShapeDtypeStruct((16, 3, 20, 16, 32), BF16),
        in_specs=[vmem, vmem],
        out_specs=pl.BlockSpec(memory_space=pl.ANY),
        scratch_shapes=[pltpu.VMEM((16, 3, 20, 16, 32), BF16), pltpu.SemaphoreType.DMA((8,))],
        compiler_params=pltpu.CompilerParams(vmem_limit_bytes=16 * 2**20),
        name="lay_out",
    )(order, arrived.reshape(2, 8, 16, 16, 128))


def body(fields, vmodes, owner_map, hough_table, keep_mask):
    arrived, order = exchange(fields, vmodes.T, owner_map.reshape(1, 16), hough_table, keep_mask)
    return lay_out(order, arrived)


def solution(mesh):
    in_specs = (P(None, None, "lat", None, "tm"), P(), P(), P("tm", "lat", None), P("tm", "lat"))
    out_specs = P(None, None, "lat", None, "tm")
    return jax.shard_map(body, mesh=mesh, in_specs=in_specs, out_specs=out_specs, check_vma=False)
```
